32 devices in a mesh: group: 2 (over x), tm: 16 (over z, y, core).
Axes of the slice: x: 2, y: 2, z: 4, core: 2. Of those that a mesh axis runs over, the one named last changes fastest.
Arguments:
- iterate: float32 [64, 2, 2, 96, 192], P(('group', 'tm')), parts along dimension 0, may hold values from 0 to 1
- labels: int32 [4, 96, 192], P('group'), parts along dimension 0, may hold values from 0 to 3
- stim_mask: int32 [4, 96, 192], P('group'), parts along dimension 0, may hold values 0 or 1
Outputs:
- corrected: float32 [64, 2, 2, 96, 192], P(('group', 'tm')), parts along dimension 0
The draws below stay inside these ranges and needn't reach their ends.
There are 2 independent parts, one for each index of `group`. The reference program is written for one: setup_inputs(seed, part) draws one part's arguments, and reference() takes and returns one part's arrays. A program takes and returns all parts, laid end to end along the dimension named above; each array names one. Nothing has to cross between parts.
All inputs are finite; a program needn't handle non-finite values.
Results may differ from the reference program's by a relative error of at most 0.0003.
Values sent between devices are 32-bit elements; how exact they have to be, the bound alone decides.
A program may use at most 256 MiB of HBM per device.

```python
import jax
import jax.numpy as jnp
from jax import lax

SX = 2
NY = 96
NZ = 192
MSTEPS = 8
PULSE = 16
SLICES = 32


def draw_iterate(key, part):
    key = jax.random.fold_in(key, 11)
    keys = jax.random.split(key, 5)
    field_shape = (SLICES, SX, NY, NZ)
    band_start = jax.random.randint(keys[0], (), 0, NY)
    band_width = max(NY // 4, 2)
    row_index = jnp.arange(NY, dtype=jnp.int32)
    in_band = ((row_index - band_start) % NY < band_width).reshape(1, 1, NY, 1)
    inner_draw = jax.random.uniform(keys[1], field_shape, jnp.float32)
    inner_recov = jax.random.uniform(keys[2], field_shape, jnp.float32)
    outer_draw = jax.random.uniform(keys[3], field_shape, jnp.float32)
    outer_recov = jax.random.uniform(keys[4], field_shape, jnp.float32)
    inner_pot = 0.1 + 0.15 * inner_draw
    inner_rec = 0.02 * inner_recov
    outer_pot = outer_draw
    outer_rec = outer_recov
    potential = jnp.where(in_band, inner_pot, outer_pot)
    recovery = jnp.where(in_band, inner_rec, outer_rec)
    return jnp.stack([potential, recovery], axis=1).astype(jnp.float32)


def place_ends(drawn, stream_key, low, top_value):
    extent = drawn.shape
    spot = [jax.random.randint(jax.random.fold_in(stream_key, axis), (), 0, extent[axis]) for axis in range(len(extent))]
    drawn = drawn.at[tuple(spot)].set(low)
    longest = extent.index(max(extent))
    spot[longest] = (spot[longest] + 1) % extent[longest]
    return drawn.at[tuple(spot)].set(top_value)


def setup_inputs(seed: int = 0, part: int = 0) -> dict:
    seeds = jax.random.split(jax.random.key(seed), 4)
    own_keys = jax.random.split(jax.random.fold_in(seeds[3], part), 4)
    iterate = draw_iterate(jax.random.fold_in(jax.random.fold_in(seeds[3], part), 71), part)
    labels = place_ends(jax.random.randint(own_keys[1], (SX, NY, NZ), 0, 4), jax.random.fold_in(own_keys[1], 1), 0, 3).astype(jnp.int32)
    stim_mask = place_ends((jax.random.randint(own_keys[2], (SX, NY, NZ), 0, 8) < 1).astype(jnp.int32), jax.random.fold_in(own_keys[2], 1), 0, 1)
    return dict(iterate=iterate, labels=labels, stim_mask=stim_mask)


time_step = 0.05
excite_gain = 8.0
threshold = 0.15
recovery_base = 0.005
recovery_gain = 0.2
recovery_shift = 0.3
pulse_height = 1.0
coarse_floor = -0.5
conduct_table = (0.1, 0.35, 0.7, 1.0)


def face_terms(labels):
    conduct = jnp.zeros(labels.shape, jnp.float32)
    for label_id, conduct_value in enumerate(conduct_table):
        conduct = conduct + jnp.where(labels == label_id, jnp.float32(conduct_value), jnp.float32(0.0))
    along_x = 0.5 * (conduct[1:] + conduct[:-1])
    along_y = 0.5 * (conduct[:, 1:] + conduct[:, :-1])
    along_z = 0.5 * (conduct[:, :, 1:] + conduct[:, :, :-1])
    return along_x, along_y, along_z


def diffuse(potential, face_coeffs):
    along_x, along_y, along_z = face_coeffs
    face_flux = along_x * (potential[1:] - potential[:-1])
    result = jnp.pad(face_flux, ((0, 1), (0, 0), (0, 0))) - jnp.pad(face_flux, ((1, 0), (0, 0), (0, 0)))
    face_flux = along_y * (potential[:, 1:] - potential[:, :-1])
    result = result + jnp.pad(face_flux, ((0, 0), (0, 1), (0, 0))) - jnp.pad(face_flux, ((0, 0), (1, 0), (0, 0)))
    face_flux = along_z * (potential[:, :, 1:] - potential[:, :, :-1])
    result = result + jnp.pad(face_flux, ((0, 0), (0, 0), (0, 1))) - jnp.pad(face_flux, ((0, 0), (0, 0), (1, 0)))
    return result


def recovery_rate(potential, recovery):
    return recovery_base + recovery_gain * jnp.maximum(recovery, 0.0) / (jnp.maximum(potential, 0.0) + recovery_shift)


def fine_update(potential, recovery, face_coeffs, stimulus, switch):
    recover_rate = recovery_rate(potential, recovery)
    source = diffuse(potential, face_coeffs) - excite_gain * potential * (potential - threshold) * (potential - 1.0)
    source = source - potential * recovery + switch * stimulus
    new_potential = potential + time_step * source
    new_recovery = recovery + time_step * recover_rate * (-recovery - excite_gain * potential * (potential - threshold - 1.0))
    return new_potential, new_recovery


def advance(c_state, face_coeffs, stimulus, first_step, beat_steps):
    def one_step(offset, running):
        moment = (first_step + offset) % beat_steps
        switch = jnp.where(moment < PULSE, 1.0, 0.0).astype(jnp.float32)
        return fine_update(running[0], running[1], face_coeffs, stimulus, switch)

    potential, recovery = lax.fori_loop(0, MSTEPS, one_step, (c_state[0], c_state[1]))
    return jnp.stack([potential, recovery])


def coarse_map(previous, relaxed):
    potential = jnp.clip(previous[0], 0.0, 1.0)
    recovery = jnp.maximum(previous[1], 0.0)
    recover_rate = recovery_rate(potential, recovery)
    horizon = MSTEPS * time_step
    fast_slope = jnp.minimum(-excite_gain * (3.0 * potential * potential - 2.0 * (1.0 + threshold) * potential + threshold) - recovery, coarse_floor)
    cross_term = -recover_rate * excite_gain * (2.0 * potential - threshold - 1.0)
    first_diag = 1.0 / (1.0 - horizon * fast_slope)
    second_diag = 1.0 / (1.0 + horizon * recover_rate)
    lower_term = horizon * cross_term * first_diag * second_diag
    residual = previous - relaxed
    return (first_diag, lower_term, second_diag, residual[0], residual[1])


def compose(earlier, latter):
    return (latter[0] * earlier[0],
            latter[1] * earlier[0] + latter[2] * earlier[1],
            latter[2] * earlier[2],
            latter[0] * earlier[3] + latter[3],
            latter[1] * earlier[3] + latter[2] * earlier[4] + latter[4])


def apply_map(mapping, first_in, second_in):
    return (mapping[0] * first_in + mapping[3], mapping[1] * first_in + mapping[2] * second_in + mapping[4])


def loop_point(loop_map):
    first_part = loop_map[3] / (1.0 - loop_map[0])
    second = (loop_map[4] + loop_map[1] * first_part) / (1.0 - loop_map[2])
    return first_part, second


def reference(iterate, labels, stim_mask):
    face_coeffs = face_terms(labels)
    stimulus = pulse_height * stim_mask.astype(jnp.float32)
    beat_steps = SLICES * MSTEPS
    step_starts = jnp.arange(SLICES, dtype=jnp.int32) * MSTEPS

    def propagate(inputs):
        return advance(inputs[0], face_coeffs, stimulus, inputs[1], beat_steps)

    predicted = lax.map(propagate, (iterate, step_starts))
    relaxed = jnp.roll(predicted, 1, axis=0)
    propagated = lax.map(propagate, (relaxed, step_starts))
    previous = jnp.roll(propagated, 1, axis=0)
    ones_field = jnp.ones(labels.shape, jnp.float32)
    zero_field = jnp.zeros(labels.shape, jnp.float32)
    identity = (ones_field, zero_field, ones_field, zero_field, zero_field)

    def gather_total(running, inputs):
        return compose(running, coarse_map(inputs[0], inputs[1])), None

    loop_map, _ = lax.scan(gather_total, identity, (previous, relaxed))
    loop_state = loop_point(loop_map)

    def sweep(running, inputs):
        correction = apply_map(coarse_map(inputs[0], inputs[1]), running[0], running[1])
        return correction, inputs[1] + jnp.stack(correction)

    _, corrected = lax.scan(sweep, loop_state, (previous, relaxed))
    return corrected
```

```python
import jax
import jax.numpy as jnp
from jax import lax
from jax.sharding import PartitionSpec as P

MSTEPS = 8
PULSE = 16


time_step = 0.05
excite_gain = 8.0
threshold = 0.15
recovery_base = 0.005
recovery_gain = 0.2
recovery_shift = 0.3
pulse_height = 1.0
coarse_floor = -0.5
conduct_table = (0.1, 0.35, 0.7, 1.0)


def from_behind(value, axis, steps):
    count = lax.axis_size(axis)
    pairs = [(source, (source + steps) % count) for source in range(count)]
    return lax.ppermute(value, axis, pairs)


def face_terms(labels):
    conduct = jnp.zeros(labels.shape, jnp.float32)
    for label_id, conduct_value in enumerate(conduct_table):
        conduct = conduct + jnp.where(
            labels == label_id, jnp.float32(conduct_value), jnp.float32(0.0)
        )
    along_x = 0.5 * (conduct[1:] + conduct[:-1])
    along_y = 0.5 * (conduct[:, 1:] + conduct[:, :-1])
    along_z = 0.5 * (conduct[:, :, 1:] + conduct[:, :, :-1])
    return (along_x, along_y, along_z)


def diffuse(potential, face_coeffs):
    along_x, along_y, along_z = face_coeffs
    face_flux = along_x * (potential[1:] - potential[:-1])
    result = jnp.pad(face_flux, ((0, 1), (0, 0), (0, 0))) - jnp.pad(
        face_flux, ((1, 0), (0, 0), (0, 0))
    )
    face_flux = along_y * (potential[:, 1:] - potential[:, :-1])
    result = (
        result
        + jnp.pad(face_flux, ((0, 0), (0, 1), (0, 0)))
        - jnp.pad(face_flux, ((0, 0), (1, 0), (0, 0)))
    )
    face_flux = along_z * (potential[:, :, 1:] - potential[:, :, :-1])
    result = (
        result
        + jnp.pad(face_flux, ((0, 0), (0, 0), (0, 1)))
        - jnp.pad(face_flux, ((0, 0), (0, 0), (1, 0)))
    )
    return result


def recovery_rate(potential, recovery):
    return recovery_base + recovery_gain * jnp.maximum(recovery, 0.0) / (
        jnp.maximum(potential, 0.0) + recovery_shift
    )


def fine_update(potential, recovery, face_coeffs, stimulus, switch):
    recover_rate = recovery_rate(potential, recovery)
    source = diffuse(potential, face_coeffs) - excite_gain * potential * (potential - threshold) * (
        potential - 1.0
    )
    source = source - potential * recovery + switch * stimulus
    new_potential = potential + time_step * source
    new_recovery = recovery + time_step * recover_rate * (
        -recovery - excite_gain * potential * (potential - threshold - 1.0)
    )
    return (new_potential, new_recovery)


def advance(c_state, face_coeffs, stimulus, first_step, beat_steps):

    def one_step(offset, running):
        moment = (first_step + offset) % beat_steps
        switch = jnp.where(moment < PULSE, 1.0, 0.0).astype(jnp.float32)
        return fine_update(running[0], running[1], face_coeffs, stimulus, switch)

    potential, recovery = lax.fori_loop(0, MSTEPS, one_step, (c_state[0], c_state[1]))
    return jnp.stack([potential, recovery])


def coarse_map(previous, relaxed):
    potential = jnp.clip(previous[0], 0.0, 1.0)
    recovery = jnp.maximum(previous[1], 0.0)
    recover_rate = recovery_rate(potential, recovery)
    horizon = MSTEPS * time_step
    fast_slope = jnp.minimum(
        -excite_gain
        * (3.0 * potential * potential - 2.0 * (1.0 + threshold) * potential + threshold)
        - recovery,
        coarse_floor,
    )
    cross_term = -recover_rate * excite_gain * (2.0 * potential - threshold - 1.0)
    first_diag = 1.0 / (1.0 - horizon * fast_slope)
    second_diag = 1.0 / (1.0 + horizon * recover_rate)
    lower_term = horizon * cross_term * first_diag * second_diag
    residual = previous - relaxed
    return (first_diag, lower_term, second_diag, residual[0], residual[1])


def compose(earlier, latter):
    return (
        latter[0] * earlier[0],
        latter[1] * earlier[0] + latter[2] * earlier[1],
        latter[2] * earlier[2],
        latter[0] * earlier[3] + latter[3],
        latter[1] * earlier[3] + latter[2] * earlier[4] + latter[4],
    )


def apply_map(mapping, first_in, second_in):
    return (
        mapping[0] * first_in + mapping[3],
        mapping[1] * first_in + mapping[2] * second_in + mapping[4],
    )


def loop_point(loop_map):
    first_part = loop_map[3] / (1.0 - loop_map[0])
    second = (loop_map[4] + loop_map[1] * first_part) / (1.0 - loop_map[2])
    return (first_part, second)


def solve_loop(own_map, size):
    shape = own_map[0].shape
    voxels = own_map[0].size
    share = -(-voxels // size)
    flat = jnp.stack(own_map).reshape(5, voxels)
    flat = jnp.pad(flat, ((0, 0), (0, share * size - voxels)))
    flat = flat.reshape(5, size, share).transpose(1, 0, 2)
    maps = lax.all_to_all(flat, "tm", 0, 0)
    maps = [[maps[k, f] for f in range(5)] for k in range(size)]
    total = maps[0]
    for mapping in maps[1:]:
        total = compose(total, mapping)
    state = loop_point(total)
    entering = []
    for mapping in maps:
        entering.append(jnp.stack(state))
        state = apply_map(mapping, state[0], state[1])
    mine = lax.all_to_all(jnp.stack(entering), "tm", 0, 0)
    mine = mine.transpose(1, 0, 2).reshape(2, size * share)[:, :voxels]
    return mine.reshape((2,) + shape)


def on_device(iterate, labels, stim_mask):
    loop_size = lax.axis_size("tm")
    slot_count = iterate.shape[0]
    first_slice = lax.axis_index("tm") * slot_count
    beat_steps = loop_size * slot_count * MSTEPS
    face_coeffs = face_terms(labels)
    stimulus = pulse_height * stim_mask.astype(jnp.float32)

    def prop(state, offset):
        return advance(state, face_coeffs, stimulus, (first_slice + offset) * MSTEPS, beat_steps)

    predicted = [None] * slot_count
    for offset in reversed(range(slot_count)):
        predicted[offset] = prop(iterate[offset], offset)
        if offset == slot_count - 1:
            incoming = from_behind(predicted[offset], "tm", 1)
    relaxed = [incoming] + predicted[:-1]
    propagated = [None] * slot_count
    for offset in reversed(range(slot_count)):
        propagated[offset] = prop(relaxed[offset], offset)
        if offset == slot_count - 1:
            arrived = from_behind(propagated[offset], "tm", 1)
    previous = [arrived] + propagated[:-1]
    slot_maps = [coarse_map(previous[offset], relaxed[offset]) for offset in range(slot_count)]
    own_map = slot_maps[0]
    for mapping in slot_maps[1:]:
        own_map = compose(own_map, mapping)
    correction = solve_loop(own_map, loop_size)
    results = []
    for offset in range(slot_count):
        correction = apply_map(slot_maps[offset], correction[0], correction[1])
        results.append(relaxed[offset] + jnp.stack(correction))
    return jnp.stack(results)


def solution(mesh):
    in_specs = (
        P(("group", "tm"), None, None, None, None),
        P("group", None, None),
        P("group", None, None),
    )
    out_specs = P(("group", "tm"), None, None, None, None)
    return jax.shard_map(
        on_device, mesh=mesh, in_specs=in_specs, out_specs=out_specs, check_vma=False
    )
```

```python
import functools

import jax
import jax.numpy as jnp
from jax import lax
from jax.experimental import pallas as pl
from jax.experimental.pallas import tpu as pltpu
from jax.sharding import PartitionSpec as P

MSTEPS = 8
PULSE = 16
LANES = 128
ROWS = 8

time_step = 0.05
excite_gain = 8.0
threshold = 0.15
recovery_base = 0.005
recovery_gain = 0.2
recovery_shift = 0.3
pulse_height = 1.0
coarse_floor = -0.5
conduct_table = (0.1, 0.35, 0.7, 1.0)


def recovery_rate(potential, recovery):
    return recovery_base + recovery_gain * jnp.maximum(recovery, 0.0) / (
        jnp.maximum(potential, 0.0) + recovery_shift
    )


def compose(earlier, latter):
    return (
        latter[0] * earlier[0],
        latter[1] * earlier[0] + latter[2] * earlier[1],
        latter[2] * earlier[2],
        latter[0] * earlier[3] + latter[3],
        latter[1] * earlier[3] + latter[2] * earlier[4] + latter[4],
    )


def apply_map(mapping, first_in, second_in):
    return (
        mapping[0] * first_in + mapping[3],
        mapping[1] * first_in + mapping[2] * second_in + mapping[4],
    )


def loop_point(loop_map):
    first_part = loop_map[3] / (1.0 - loop_map[0])
    second = (loop_map[4] + loop_map[1] * first_part) / (1.0 - loop_map[2])
    return (first_part, second)


def neighbours(ref, slot, tile, lane):
    here = pl.ds(ROWS + ROWS * tile, ROWS)
    above = pl.ds(ROWS - 1 + ROWS * tile, ROWS)
    below = pl.ds(ROWS + 1 + ROWS * tile, ROWS)
    mid = [ref[slot, k, here] for k in range(3)]
    up = [ref[slot, k, above] for k in range(3)]
    down = [ref[slot, k, below] for k in range(3)]
    first, second, rest = mid
    swapped = pltpu.roll(rest, 64, 1)
    first_left = pltpu.roll(first, 1, 1)
    rest_right = pltpu.roll(rest, LANES - 1, 1)
    left = [
        first_left,
        pltpu.roll(second, 1, 1),
        jnp.where(
            lane == 0,
            first_left,
            jnp.where(lane == 64, pltpu.roll(second, 65, 1), pltpu.roll(rest, 1, 1)),
        ),
    ]
    right = [
        jnp.where(lane == LANES - 1, rest_right, pltpu.roll(first, LANES - 1, 1)),
        jnp.where(
            lane == LANES - 1,
            pltpu.roll(swapped, LANES - 1, 1),
            pltpu.roll(second, LANES - 1, 1),
        ),
        rest_right,
    ]
    return mid, up, down, left, right, [second, first, swapped]


def slot_map(prev_p, prev_q, relax_p, relax_q):
    potential = jnp.clip(prev_p, 0.0, 1.0)
    recovery = jnp.maximum(prev_q, 0.0)
    recover_rate = recovery_rate(potential, recovery)
    horizon = MSTEPS * time_step
    fast_slope = jnp.minimum(
        -excite_gain
        * (3.0 * potential * potential - 2.0 * (1.0 + threshold) * potential + threshold)
        - recovery,
        coarse_floor,
    )
    cross_term = -recover_rate * excite_gain * (2.0 * potential - threshold - 1.0)
    first_diag = 1.0 / (1.0 - horizon * fast_slope)
    second_diag = 1.0 / (1.0 + horizon * recover_rate)
    lower_term = horizon * cross_term * first_diag * second_diag
    return (first_diag, lower_term, second_diag, prev_p - relax_p, prev_q - relax_q)


def kernel(
    loop_size, chips, groups,
    it_ref, conduct_ref, stim_ref, out_ref,
    pot, rec, cond, coef, relaxed, previous, sent, maps, own, got, early, pair,
    parts, total, totals, leave, enter, pass_on, entry,
    ring_s, ring_r, a_s, a_r, b_s, b_r, g_s, g_r, c_s, c_r, d_s, d_r,
):
    slots = it_ref.shape[0]
    tiles = conduct_ref.shape[1] // ROWS
    half = tiles // 2
    me = lax.axis_index("tm")
    core = lax.rem(me, 2)
    chip = lax.rem(me // 2, chips)
    group = me // (2 * chips)
    base = group * 2 * chips
    partner = me + 1 - 2 * core
    right = lax.rem(me + 1, loop_size)
    across = lax.rem(me + 2 * core - 1 + loop_size, loop_size)
    owner = jnp.logical_and(chip != 1, chip != chips - 2)
    my_tile = chip - (chip + chips - 1) // chips - (chip + 2) // chips

    barrier = pltpu.get_barrier_semaphore()

    def greet(device):
        pl.semaphore_signal(
            barrier, inc=1, device_id={"tm": device}, device_id_type=pl.DeviceIdType.MESH
        )

    greet(partner)
    greet(across)
    for hop in range(1, chips):
        greet(base + 2 * lax.rem(chip + hop, chips) + core)
    for hop in range(1, groups):
        greet(lax.rem(me + hop * 2 * chips, loop_size))

    def remote(source, target, send_sem, recv_sem, device):
        return pltpu.make_async_remote_copy(
            src_ref=source, dst_ref=target, send_sem=send_sem, recv_sem=recv_sem,
            device_id={"tm": device}, device_id_type=pl.DeviceIdType.MESH,
        )

    lane = lax.broadcasted_iota(jnp.int32, (ROWS, LANES), 1)
    row = lax.broadcasted_iota(jnp.int32, (ROWS, LANES), 0)
    edge = jnp.zeros((ROWS, LANES), jnp.float32)
    for k in range(3):
        for end in (0, ROWS + ROWS * tiles):
            cond[0, k, pl.ds(end, ROWS)] = edge
            pot[0, k, pl.ds(end, ROWS)] = edge
            pot[1, k, pl.ds(end, ROWS)] = edge
        cond[0, k, pl.ds(ROWS, ROWS * tiles)] = conduct_ref[k]
    for t in range(tiles):
        mid, up, down, left, right_, over = neighbours(cond, 0, t, lane)
        here = pl.ds(ROWS * t, ROWS)
        for k in range(3):
            def face(value, open_face=None):
                mean = time_step * 0.5 * (mid[k] + value)
                return mean if open_face is None else jnp.where(open_face, mean, 0.0)

            faces = (
                face(up[k], row > 0 if t == 0 else None),
                face(down[k], row < ROWS - 1 if t == tiles - 1 else None),
                face(left[k], lane > 0 if k < 2 else None),
                face(
                    right_[k],
                    None if k < 2 else jnp.logical_and(lane != 63, lane != LANES - 1),
                ),
                face(over[k]),
            )
            for n, value in enumerate(faces):
                coef[n, k, here] = value
            coef[5, k, here] = 1.0 - (((faces[0] + faces[1]) + (faces[2] + faces[3])) + faces[4])

    def advance(source, target, slice_index):
        for k in range(3):
            pot[0, k, pl.ds(ROWS, ROWS * tiles)] = source[0, k]
            rec[k] = source[1, k]

        def one_step(step, carry):
            moment = lax.rem(slice_index * MSTEPS + step, loop_size * slots * MSTEPS)
            switch = jnp.where(moment < PULSE, time_step * pulse_height, 0.0)
            now = lax.rem(step, 2)
            for t in range(tiles):
                mid, up, down, left, right_, over = neighbours(pot, now, t, lane)
                here = pl.ds(ROWS * t, ROWS)
                for k in range(3):
                    p, q = mid[k], rec[k, here]
                    flow = coef[0, k, here] * up[k] + coef[1, k, here] * down[k]
                    flow = flow + (coef[2, k, here] * left[k] + coef[3, k, here] * right_[k])
                    flow = flow + (coef[4, k, here] * over[k] + switch * stim_ref[k, here])
                    gain = (p - threshold) * (p - 1.0)
                    keep = coef[5, k, here] - time_step * (excite_gain * gain + q)
                    pot[1 - now, k, pl.ds(ROWS + ROWS * t, ROWS)] = p * keep + flow
                    rate = time_step * recovery_rate(p, q)
                    pull = q + excite_gain * p * (p - (threshold + 1.0))
                    rec[k, here] = q - rate * pull
            return carry

        lax.fori_loop(0, MSTEPS, one_step, 0)
        for k in range(3):
            target[0, k] = pot[MSTEPS % 2, k, pl.ds(ROWS, ROWS * tiles)]
            target[1, k] = rec[k]

    first_slice = me * slots
    last = slots - 1
    advance(it_ref.at[last], sent.at[0], first_slice + last)
    pl.semaphore_wait(barrier, chips + 1 + groups - 1)
    ring_one = remote(sent.at[0], relaxed.at[0], ring_s.at[0], ring_r.at[0], right)
    ring_one.start()
    for s in reversed(range(last)):
        advance(it_ref.at[s], relaxed.at[s + 1], first_slice + s)
    ring_two = remote(sent.at[1], previous.at[0], ring_s.at[1], ring_r.at[1], right)
    for s in reversed(range(slots)):
        if s == 0:
            ring_one.wait_recv()
        if s == last:
            advance(relaxed.at[s], sent.at[1], first_slice + s)
            ring_two.start()
        else:
            advance(relaxed.at[s], previous.at[s + 1], first_slice + s)
    ring_two.wait_recv()

    def make_maps(t):
        here = pl.ds(pl.multiple_of(ROWS * t, ROWS), ROWS)
        for k in range(3):
            whole = None
            for s in range(slots):
                mapping = slot_map(
                    previous[s, 0, k, here], previous[s, 1, k, here],
                    relaxed[s, 0, k, here], relaxed[s, 1, k, here],
                )
                for n in range(5):
                    maps[s, t, n, k] = mapping[n]
                whole = mapping if whole is None else compose(whole, mapping)
            for n in range(5):
                own[t, n, k] = whole[n]

    def fields(ref, *place):
        return tuple(ref[(*place, n)] for n in range(5))

    def a_copy(j):
        return remote(
            own.at[half * (1 - core) + j], got.at[j], a_s.at[j], a_r.at[j], partner
        )

    def phase_send(j, carry):
        make_maps(half * (1 - core) + j)
        a_copy(j).start()
        return carry

    def phase_keep(j, carry):
        make_maps(half * core + j)
        return carry

    lax.fori_loop(0, half, phase_send, 0)
    lax.fori_loop(0, half, phase_keep, 0)

    def owner_of(j):
        return j + (j + half - 1) // half + (j + 1) // half

    def b_copy(j):
        return remote(
            pair.at[j], parts.at[chip], b_s.at[j], b_r.at[chip],
            base + 2 * owner_of(j) + core,
        )

    def phase_pair(turn, carry):
        j = lax.rem(turn + chip, half)
        a_copy(j).wait_recv()
        for k in range(3):
            mine = tuple(own[half * core + j, n, k] for n in range(5))
            theirs = tuple(got[j, n, k] for n in range(5))
            is_first = core == 0
            earlier = tuple(jnp.where(is_first, m, h) for m, h in zip(mine, theirs))
            later = tuple(jnp.where(is_first, h, m) for m, h in zip(mine, theirs))
            both = compose(earlier, later)
            for n in range(5):
                early[j, n, k] = earlier[n]
                pair[j, n, k] = both[n]

        @pl.when(owner_of(j) != chip)
        def _():
            b_copy(j).start()

        @pl.when(owner_of(j) == chip)
        def _():
            parts[chip] = pair[j]

        return carry

    lax.fori_loop(0, half, phase_pair, 0)

    def c_copy(k):
        return remote(
            leave.at[k], enter.at[my_tile], c_s.at[k], c_r.at[my_tile], base + 2 * k + core
        )

    @pl.when(owner)
    def _():
        for k in range(chips):
            @pl.when(chip != k)
            def _():
                remote(
                    pair.at[0], parts.at[k], b_s.at[0], b_r.at[k], base + 2 * k + core
                ).wait_recv()

        whole = fields(parts, 0)
        for k in range(1, chips):
            whole = compose(whole, fields(parts, k))
        if groups == 1:
            state = loop_point(whole)
        else:
            total[...] = jnp.stack(whole)
            totals[group] = total[...]

            def g_copy(hop):
                to = lax.rem(me + hop * 2 * chips, loop_size)
                return remote(total, totals.at[group], g_s.at[hop], g_r.at[hop], to)

            for hop in range(1, groups):
                g_copy(hop).start()
            for hop in range(1, groups):
                g_copy(hop).wait()
            whole = fields(totals, 0)
            for g in range(1, groups):
                whole = compose(whole, fields(totals, g))
            state = loop_point(whole)
            for g in range(groups - 1):
                after = apply_map(fields(totals, g), state[0], state[1])
                state = tuple(jnp.where(g < group, n, o) for n, o in zip(after, state))
        for k in range(chips):
            leave[k, 0] = state[0]
            leave[k, 1] = state[1]

            @pl.when(chip != k)
            def _():
                c_copy(k).start()

            @pl.when(chip == k)
            def _():
                enter[my_tile] = leave[k]

            if k < chips - 1:
                state = apply_map(fields(parts, k), state[0], state[1])

    def finish(t):
        here = pl.ds(pl.multiple_of(ROWS * t, ROWS), ROWS)
        for k in range(3):
            value = (entry[t, 0, k], entry[t, 1, k])
            for s in range(slots):
                mapping = tuple(maps[s, t, n, k] for n in range(5))
                value = apply_map(mapping, value[0], value[1])
                out_ref[s, 0, k, here] = relaxed[s, 0, k, here] + value[0]
                out_ref[s, 1, k, here] = relaxed[s, 1, k, here] + value[1]

    def d_copy(j):
        return remote(pass_on.at[j], entry.at[half * core + j], d_s.at[j], d_r.at[j], partner)

    def phase_back(j, carry):
        @pl.when(owner_of(j) != chip)
        def _():
            remote(
                leave.at[0], enter.at[j], c_s.at[0], c_r.at[j], base + 2 * owner_of(j) + core
            ).wait_recv()

        for k in range(3):
            zero = (enter[j, 0, k], enter[j, 1, k])
            one = apply_map(tuple(early[j, n, k] for n in range(5)), zero[0], zero[1])
            for n in range(2):
                entry[half * core + j, n, k] = jnp.where(core == 0, zero[n], one[n])
                pass_on[j, n, k] = jnp.where(core == 0, one[n], zero[n])
        d_copy(j).start()
        return carry

    lax.fori_loop(0, half, phase_back, 0)

    def phase_mine(j, carry):
        finish(half * core + j)
        return carry

    def phase_theirs(j, carry):
        remote(
            pass_on.at[j], entry.at[half * (1 - core) + j], d_s.at[j], d_r.at[j], partner
        ).wait_recv()
        finish(half * (1 - core) + j)
        return carry

    lax.fori_loop(0, half, phase_mine, 0)
    lax.fori_loop(0, half, phase_theirs, 0)

    ring_one.wait_send()
    ring_two.wait_send()
    for j in range(half):
        a_copy(j).wait_send()
        d_copy(j).wait_send()

        @pl.when(owner_of(j) != chip)
        def _():
            b_copy(j).wait_send()

    @pl.when(owner)
    def _():
        for k in range(chips):
            @pl.when(chip != k)
            def _():
                c_copy(k).wait_send()


def pack(field):
    rest = field[..., LANES:]
    rest = jnp.concatenate([rest[..., 0, :, :], rest[..., 1, :, :]], axis=-1)
    return jnp.concatenate([field[..., :LANES], rest[..., None, :, :]], axis=-3)


def unpack(packed):
    rest = packed[..., 2, :, :]
    rest = jnp.stack([rest[..., : LANES // 2], rest[..., LANES // 2 :]], axis=-3)
    return jnp.concatenate([packed[..., :2, :, :], rest], axis=-1)


def on_device(iterate, labels, stim_mask):
    loop_size = lax.axis_size("tm")
    chips = 8
    groups = loop_size // (2 * chips)
    slots = iterate.shape[0]
    conduct = jnp.zeros(labels.shape, jnp.float32)
    for label_id, conduct_value in enumerate(conduct_table):
        conduct = jnp.where(labels == label_id, jnp.float32(conduct_value), conduct)
    state = pack(iterate)
    rows = labels.shape[1]
    tiles = rows // ROWS
    half = tiles // 2
    f32 = jnp.float32
    block = (3, ROWS, LANES)
    dma = pltpu.SemaphoreType.DMA
    out = pl.pallas_call(
        functools.partial(kernel, loop_size, chips, groups),
        out_shape=jax.ShapeDtypeStruct(state.shape, f32),
        in_specs=[pl.BlockSpec(memory_space=pltpu.VMEM)] * 3,
        out_specs=pl.BlockSpec(memory_space=pltpu.VMEM),
        scratch_shapes=[
            pltpu.VMEM((2, 3, rows + 2 * ROWS, LANES), f32),
            pltpu.VMEM((3, rows, LANES), f32),
            pltpu.VMEM((1, 3, rows + 2 * ROWS, LANES), f32),
            pltpu.VMEM((6, 3, rows, LANES), f32),
            pltpu.VMEM(state.shape, f32),
            pltpu.VMEM(state.shape, f32),
            pltpu.VMEM((2, 2, 3, rows, LANES), f32),
            pltpu.VMEM((slots, tiles, 5) + block, f32),
            pltpu.VMEM((tiles, 5) + block, f32),
            pltpu.VMEM((half, 5) + block, f32),
            pltpu.VMEM((half, 5) + block, f32),
            pltpu.VMEM((half, 5) + block, f32),
            pltpu.VMEM((chips, 5) + block, f32),
            pltpu.VMEM((5,) + block, f32),
            pltpu.VMEM((groups, 5) + block, f32),
            pltpu.VMEM((chips, 2) + block, f32),
            pltpu.VMEM((half, 2) + block, f32),
            pltpu.VMEM((half, 2) + block, f32),
            pltpu.VMEM((tiles, 2) + block, f32),
            dma((2,)), dma((2,)),
            dma((half,)), dma((half,)),
            dma((half,)), dma((chips,)),
            dma((groups,)), dma((groups,)),
            dma((chips,)), dma((half,)),
            dma((half,)), dma((half,)),
        ],
        compiler_params=pltpu.CompilerParams(
            collective_id=0, has_side_effects=True, vmem_limit_bytes=32 * 1024 * 1024
        ),
    )(state, pack(conduct), pack(stim_mask.astype(f32)))
    return unpack(out)


def solution(mesh):
    in_specs = (
        P(("group", "tm"), None, None, None, None),
        P("group", None, None),
        P("group", None, None),
    )
    out_specs = P(("group", "tm"), None, None, None, None)
    return jax.shard_map(
        on_device, mesh=mesh, in_specs=in_specs, out_specs=out_specs, check_vma=False
    )
```

```python
import functools

import jax
import jax.numpy as jnp
from jax import lax
from jax.experimental import pallas as pl
from jax.experimental.pallas import tpu as pltpu
from jax.sharding import PartitionSpec as P

MSTEPS = 8
PULSE = 16
LANES = 128
ROWS = 8

time_step = 0.05
excite_gain = 8.0
threshold = 0.15
recovery_base = 0.005
recovery_gain = 0.2
recovery_shift = 0.3
pulse_height = 1.0
coarse_floor = -0.5
conduct_table = (0.1, 0.35, 0.7, 1.0)


def inverse(value):
    guess = pl.reciprocal(value, approx=True)
    return guess * (2.0 - value * guess)


def scaled_rate(potential, recovery, scale):
    above = (scale * recovery_gain) * jnp.maximum(recovery, 0.0)
    return scale * recovery_base + above * inverse(jnp.maximum(potential, 0.0) + recovery_shift)


def compose(earlier, latter):
    return (
        latter[0] * earlier[0],
        latter[1] * earlier[0] + latter[2] * earlier[1],
        latter[2] * earlier[2],
        latter[0] * earlier[3] + latter[3],
        latter[1] * earlier[3] + latter[2] * earlier[4] + latter[4],
    )


def apply_map(mapping, first_in, second_in):
    return (
        mapping[0] * first_in + mapping[3],
        mapping[1] * first_in + mapping[2] * second_in + mapping[4],
    )


def loop_point(loop_map):
    first_part = loop_map[3] / (1.0 - loop_map[0])
    second = (loop_map[4] + loop_map[1] * first_part) / (1.0 - loop_map[2])
    return (first_part, second)


def neighbours(ref, slot, tile, lane):
    here = pl.ds(ROWS + ROWS * tile, ROWS)
    above = pl.ds(ROWS - 1 + ROWS * tile, ROWS)
    below = pl.ds(ROWS + 1 + ROWS * tile, ROWS)
    mid = [ref[slot, k, here] for k in range(3)]
    up = [ref[slot, k, above] for k in range(3)]
    down = [ref[slot, k, below] for k in range(3)]
    first, second, rest = mid
    swapped = pltpu.roll(rest, 64, 1)
    first_left = pltpu.roll(first, 1, 1)
    rest_right = pltpu.roll(rest, LANES - 1, 1)
    left = [
        first_left,
        pltpu.roll(second, 1, 1),
        jnp.where(
            lane == 0,
            first_left,
            jnp.where(lane == 64, pltpu.roll(second, 65, 1), pltpu.roll(rest, 1, 1)),
        ),
    ]
    right = [
        jnp.where(lane == LANES - 1, rest_right, pltpu.roll(first, LANES - 1, 1)),
        jnp.where(
            lane == LANES - 1,
            pltpu.roll(swapped, LANES - 1, 1),
            pltpu.roll(second, LANES - 1, 1),
        ),
        rest_right,
    ]
    return mid, up, down, left, right, [second, first, swapped]


def packed(ref, place, here):
    first, second = ref[(*place, 0, here)], ref[(*place, 1, here)]
    rest = jnp.concatenate([first[:, LANES:], second[:, LANES:]], axis=1)
    return [first[:, :LANES], second[:, :LANES], rest]


def slot_map(prev_p, prev_q, relax_p, relax_q):
    potential = jnp.clip(prev_p, 0.0, 1.0)
    recovery = jnp.maximum(prev_q, 0.0)
    recover_rate = scaled_rate(potential, recovery, 1.0)
    horizon = MSTEPS * time_step
    fast_slope = jnp.minimum(
        -excite_gain
        * (3.0 * potential * potential - 2.0 * (1.0 + threshold) * potential + threshold)
        - recovery,
        coarse_floor,
    )
    cross_term = -recover_rate * excite_gain * (2.0 * potential - threshold - 1.0)
    first_diag = inverse(1.0 - horizon * fast_slope)
    second_diag = inverse(1.0 + horizon * recover_rate)
    lower_term = horizon * cross_term * first_diag * second_diag
    return (first_diag, lower_term, second_diag, prev_p - relax_p, prev_q - relax_q)


def kernel(
    loop_size, chips, groups,
    iterate_hbm, labels_hbm, stim_hbm, out_ref,
    raw, raw_labels, raw_stim, it_ref, stim_ref, load_sem,
    pot, rec, drive, cond, coef, relaxed, previous, sent, maps, own, got, early, pair,
    parts, total, totals, leave, enter, pass_on, entry,
    ring_s, ring_r, a_s, a_r, b_s, b_r, g_s, g_r, c_s, c_r, d_s, d_r,
):
    slots = it_ref.shape[0]
    tiles = stim_ref.shape[1] // ROWS
    last = slots - 1
    loads = [
        pltpu.make_async_copy(labels_hbm, raw_labels, load_sem.at[slots]),
        pltpu.make_async_copy(stim_hbm, raw_stim, load_sem.at[slots + 1]),
    ]
    for s in reversed(range(slots)):
        loads.append(pltpu.make_async_copy(iterate_hbm.at[s], raw.at[s], load_sem.at[s]))
    for load in loads:
        load.start()
    half = tiles // 2
    me = lax.axis_index("tm")
    core = lax.rem(me, 2)
    chip = lax.rem(me // 2, chips)
    group = me // (2 * chips)
    base = group * 2 * chips
    partner = me + 1 - 2 * core
    right = lax.rem(me + 1, loop_size)
    across = lax.rem(me + 2 * core - 1 + loop_size, loop_size)
    owner = jnp.logical_and(chip != 1, chip != chips - 2)
    my_tile = chip - (chip + chips - 1) // chips - (chip + 2) // chips

    barrier = pltpu.get_barrier_semaphore()

    def greet(device):
        pl.semaphore_signal(
            barrier, inc=1, device_id={"tm": device}, device_id_type=pl.DeviceIdType.MESH
        )

    greet(partner)
    greet(across)
    for hop in range(1, chips):
        greet(base + 2 * lax.rem(chip + hop, chips) + core)
    for hop in range(1, groups):
        greet(lax.rem(me + hop * 2 * chips, loop_size))

    def remote(source, target, send_sem, recv_sem, device):
        return pltpu.make_async_remote_copy(
            src_ref=source, dst_ref=target, send_sem=send_sem, recv_sem=recv_sem,
            device_id={"tm": device}, device_id_type=pl.DeviceIdType.MESH,
        )

    lane = lax.broadcasted_iota(jnp.int32, (ROWS, LANES), 1)
    row = lax.broadcasted_iota(jnp.int32, (ROWS, LANES), 0)
    edge = jnp.zeros((ROWS, LANES), jnp.float32)
    for k in range(3):
        for end in (0, ROWS + ROWS * tiles):
            cond[0, k, pl.ds(end, ROWS)] = edge
            pot[0, k, pl.ds(end, ROWS)] = edge
            pot[1, k, pl.ds(end, ROWS)] = edge
    loads[0].wait()
    for t in range(tiles):
        here = pl.ds(ROWS * t, ROWS)
        for k, label in enumerate(packed(raw_labels, (), here)):
            conduct = jnp.full((ROWS, LANES), conduct_table[0], jnp.float32)
            for label_id in range(1, len(conduct_table)):
                conduct = jnp.where(label == label_id, conduct_table[label_id], conduct)
            cond[0, k, pl.ds(ROWS + ROWS * t, ROWS)] = conduct
    loads[1].wait()
    for t in range(tiles):
        here = pl.ds(ROWS * t, ROWS)
        for k, mask in enumerate(packed(raw_stim, (), here)):
            stim_ref[k, here] = mask.astype(jnp.float32)
    for t in range(tiles):
        mid, up, down, left, right_, over = neighbours(cond, 0, t, lane)
        here = pl.ds(ROWS * t, ROWS)
        for k in range(3):
            def face(value, open_face=None):
                mean = time_step * 0.5 * (mid[k] + value)
                return mean if open_face is None else jnp.where(open_face, mean, 0.0)

            faces = (
                face(up[k], row > 0 if t == 0 else None),
                face(down[k], row < ROWS - 1 if t == tiles - 1 else None),
                face(left[k], lane > 0 if k < 2 else None),
                face(
                    right_[k],
                    None if k < 2 else jnp.logical_and(lane != 63, lane != LANES - 1),
                ),
                face(over[k]),
            )
            for n, value in enumerate(faces):
                coef[n, k, here] = value
            stay = 1.0 - time_step * excite_gain * threshold
            coef[5, k, here] = stay - (((faces[0] + faces[1]) + (faces[2] + faces[3])) + faces[4])

    def unload(s):
        loads[2 + last - s].wait()
        for n in range(2):
            for t in range(tiles):
                here = pl.ds(ROWS * t, ROWS)
                for k, value in enumerate(packed(raw, (s, n), here)):
                    it_ref[s, n, k, here] = value

    def advance(source, target, slice_index):
        switch = jnp.where(slice_index * MSTEPS < PULSE, time_step * pulse_height, 0.0)
        for k in range(3):
            pot[0, k, pl.ds(ROWS, ROWS * tiles)] = source[0, k]
            rec[k] = source[1, k]
            drive[k] = switch * stim_ref[k]

        def one_step(step, carry):
            now = lax.rem(step, 2)
            for t in range(tiles):
                mid, up, down, left, right_, over = neighbours(pot, now, t, lane)
                here = pl.ds(ROWS * t, ROWS)
                for k in range(3):
                    p, q = mid[k], rec[k, here]
                    flow = coef[0, k, here] * up[k] + coef[1, k, here] * down[k]
                    flow = flow + (coef[2, k, here] * left[k] + coef[3, k, here] * right_[k])
                    flow = flow + (coef[4, k, here] * over[k] + drive[k, here])
                    pull = q + excite_gain * (p * (p - (threshold + 1.0)))
                    keep = coef[5, k, here] - time_step * pull
                    pot[1 - now, k, pl.ds(ROWS + ROWS * t, ROWS)] = p * keep + flow
                    rec[k, here] = q - scaled_rate(p, q, time_step) * pull
            return carry

        lax.fori_loop(0, MSTEPS, one_step, 0)
        for k in range(3):
            target[0, k] = pot[MSTEPS % 2, k, pl.ds(ROWS, ROWS * tiles)]
            target[1, k] = rec[k]

    first_slice = me * slots
    unload(last)
    advance(it_ref.at[last], sent.at[0], first_slice + last)
    pl.semaphore_wait(barrier, chips + 1 + groups - 1)
    ring_one = remote(sent.at[0], relaxed.at[0], ring_s.at[0], ring_r.at[0], right)
    ring_one.start()
    for s in reversed(range(last)):
        unload(s)
        advance(it_ref.at[s], relaxed.at[s + 1], first_slice + s)
    ring_two = remote(sent.at[1], previous.at[0], ring_s.at[1], ring_r.at[1], right)
    for s in reversed(range(slots)):
        if s == 0:
            ring_one.wait_recv()
        if s == last:
            advance(relaxed.at[s], sent.at[1], first_slice + s)
            ring_two.start()
        else:
            advance(relaxed.at[s], previous.at[s + 1], first_slice + s)
    ring_two.wait_recv()

    def make_maps(t):
        here = pl.ds(pl.multiple_of(ROWS * t, ROWS), ROWS)
        for k in range(3):
            whole = None
            for s in range(slots):
                mapping = slot_map(
                    previous[s, 0, k, here], previous[s, 1, k, here],
                    relaxed[s, 0, k, here], relaxed[s, 1, k, here],
                )
                for n in range(5):
                    maps[s, t, n, k] = mapping[n]
                whole = mapping if whole is None else compose(whole, mapping)
            for n in range(5):
                own[t, n, k] = whole[n]

    def fields(ref, *place):
        return tuple(ref[(*place, n)] for n in range(5))

    def a_copy(j):
        return remote(
            own.at[half * (1 - core) + j], got.at[j], a_s.at[j], a_r.at[j], partner
        )

    def phase_send(j, carry):
        make_maps(half * (1 - core) + j)
        a_copy(j).start()
        return carry

    def phase_keep(j, carry):
        make_maps(half * core + j)
        return carry

    lax.fori_loop(0, half, phase_send, 0)
    lax.fori_loop(0, half, phase_keep, 0)

    def owner_of(j):
        return j + (j + half - 1) // half + (j + 1) // half

    def b_copy(j):
        return remote(
            pair.at[j], parts.at[chip], b_s.at[j], b_r.at[chip],
            base + 2 * owner_of(j) + core,
        )

    def phase_pair(turn, carry):
        j = lax.rem(turn + chip, half)
        a_copy(j).wait_recv()
        for k in range(3):
            mine = tuple(own[half * core + j, n, k] for n in range(5))
            theirs = tuple(got[j, n, k] for n in range(5))
            is_first = core == 0
            earlier = tuple(jnp.where(is_first, m, h) for m, h in zip(mine, theirs))
            later = tuple(jnp.where(is_first, h, m) for m, h in zip(mine, theirs))
            both = compose(earlier, later)
            for n in range(5):
                early[j, n, k] = earlier[n]
                pair[j, n, k] = both[n]

        @pl.when(owner_of(j) != chip)
        def _():
            b_copy(j).start()

        @pl.when(owner_of(j) == chip)
        def _():
            parts[chip] = pair[j]

        return carry

    lax.fori_loop(0, half, phase_pair, 0)

    def c_copy(k):
        return remote(
            leave.at[k], enter.at[my_tile], c_s.at[k], c_r.at[my_tile], base + 2 * k + core
        )

    @pl.when(owner)
    def _():
        for k in range(chips):
            @pl.when(chip != k)
            def _():
                remote(
                    pair.at[0], parts.at[k], b_s.at[0], b_r.at[k], base + 2 * k + core
                ).wait_recv()

        whole = fields(parts, 0)
        for k in range(1, chips):
            whole = compose(whole, fields(parts, k))
        if groups == 1:
            state = loop_point(whole)
        else:
            total[...] = jnp.stack(whole)
            totals[group] = total[...]

            def g_copy(hop):
                to = lax.rem(me + hop * 2 * chips, loop_size)
                return remote(total, totals.at[group], g_s.at[hop], g_r.at[hop], to)

            for hop in range(1, groups):
                g_copy(hop).start()
            for hop in range(1, groups):
                g_copy(hop).wait()
            whole = fields(totals, 0)
            for g in range(1, groups):
                whole = compose(whole, fields(totals, g))
            state = loop_point(whole)
            for g in range(groups - 1):
                after = apply_map(fields(totals, g), state[0], state[1])
                state = tuple(jnp.where(g < group, n, o) for n, o in zip(after, state))
        for k in range(chips):
            leave[k, 0] = state[0]
            leave[k, 1] = state[1]

            @pl.when(chip != k)
            def _():
                c_copy(k).start()

            @pl.when(chip == k)
            def _():
                enter[my_tile] = leave[k]

            if k < chips - 1:
                state = apply_map(fields(parts, k), state[0], state[1])

    def finish(t):
        here = pl.ds(pl.multiple_of(ROWS * t, ROWS), ROWS)
        for k in range(3):
            value = (entry[t, 0, k], entry[t, 1, k])
            for s in range(slots):
                mapping = tuple(maps[s, t, n, k] for n in range(5))
                value = apply_map(mapping, value[0], value[1])
                out_ref[s, 0, k, here] = relaxed[s, 0, k, here] + value[0]
                out_ref[s, 1, k, here] = relaxed[s, 1, k, here] + value[1]

    def d_copy(j):
        return remote(pass_on.at[j], entry.at[half * core + j], d_s.at[j], d_r.at[j], partner)

    def phase_back(j, carry):
        @pl.when(owner_of(j) != chip)
        def _():
            remote(
                leave.at[0], enter.at[j], c_s.at[0], c_r.at[j], base + 2 * owner_of(j) + core
            ).wait_recv()

        for k in range(3):
            zero = (enter[j, 0, k], enter[j, 1, k])
            one = apply_map(tuple(early[j, n, k] for n in range(5)), zero[0], zero[1])
            for n in range(2):
                entry[half * core + j, n, k] = jnp.where(core == 0, zero[n], one[n])
                pass_on[j, n, k] = jnp.where(core == 0, one[n], zero[n])
        d_copy(j).start()
        return carry

    lax.fori_loop(0, half, phase_back, 0)

    def phase_mine(j, carry):
        finish(half * core + j)
        return carry

    def phase_theirs(j, carry):
        remote(
            pass_on.at[j], entry.at[half * (1 - core) + j], d_s.at[j], d_r.at[j], partner
        ).wait_recv()
        finish(half * (1 - core) + j)
        return carry

    lax.fori_loop(0, half, phase_mine, 0)
    lax.fori_loop(0, half, phase_theirs, 0)

    ring_one.wait_send()
    ring_two.wait_send()
    for j in range(half):
        a_copy(j).wait_send()
        d_copy(j).wait_send()

        @pl.when(owner_of(j) != chip)
        def _():
            b_copy(j).wait_send()

    @pl.when(owner)
    def _():
        for k in range(chips):
            @pl.when(chip != k)
            def _():
                c_copy(k).wait_send()


def unpack(packed):
    rest = packed[..., 2, :, :]
    rest = jnp.stack([rest[..., : LANES // 2], rest[..., LANES // 2 :]], axis=-3)
    return jnp.concatenate([packed[..., :2, :, :], rest], axis=-1)


def on_device(iterate, labels, stim_mask):
    loop_size = lax.axis_size("tm")
    chips = 8
    groups = loop_size // (2 * chips)
    slots = iterate.shape[0]
    rows = labels.shape[1]
    tiles = rows // ROWS
    half = tiles // 2
    f32 = jnp.float32
    state = (slots, 2, 3, rows, LANES)
    block = (3, ROWS, LANES)
    dma = pltpu.SemaphoreType.DMA
    out = pl.pallas_call(
        functools.partial(kernel, loop_size, chips, groups),
        out_shape=jax.ShapeDtypeStruct(state, f32),
        in_specs=[pl.BlockSpec(memory_space=pl.ANY)] * 3,
        out_specs=pl.BlockSpec(memory_space=pltpu.VMEM),
        scratch_shapes=[
            pltpu.VMEM(iterate.shape, f32),
            pltpu.VMEM(labels.shape, labels.dtype),
            pltpu.VMEM(stim_mask.shape, stim_mask.dtype),
            pltpu.VMEM(state, f32),
            pltpu.VMEM((3, rows, LANES), f32),
            pltpu.SemaphoreType.DMA((slots + 2,)),
            pltpu.VMEM((2, 3, rows + 2 * ROWS, LANES), f32),
            pltpu.VMEM((3, rows, LANES), f32),
            pltpu.VMEM((3, rows, LANES), f32),
            pltpu.VMEM((1, 3, rows + 2 * ROWS, LANES), f32),
            pltpu.VMEM((6, 3, rows, LANES), f32),
            pltpu.VMEM(state, f32),
            pltpu.VMEM(state, f32),
            pltpu.VMEM((2, 2, 3, rows, LANES), f32),
            pltpu.VMEM((slots, tiles, 5) + block, f32),
            pltpu.VMEM((tiles, 5) + block, f32),
            pltpu.VMEM((half, 5) + block, f32),
            pltpu.VMEM((half, 5) + block, f32),
            pltpu.VMEM((half, 5) + block, f32),
            pltpu.VMEM((chips, 5) + block, f32),
            pltpu.VMEM((5,) + block, f32),
            pltpu.VMEM((groups, 5) + block, f32),
            pltpu.VMEM((chips, 2) + block, f32),
            pltpu.VMEM((half, 2) + block, f32),
            pltpu.VMEM((half, 2) + block, f32),
            pltpu.VMEM((tiles, 2) + block, f32),
            dma((2,)), dma((2,)),
            dma((half,)), dma((half,)),
            dma((half,)), dma((chips,)),
            dma((groups,)), dma((groups,)),
            dma((chips,)), dma((half,)),
            dma((half,)), dma((half,)),
        ],
        compiler_params=pltpu.CompilerParams(
            collective_id=0, has_side_effects=True, vmem_limit_bytes=32 * 1024 * 1024
        ),
    )(iterate, labels, stim_mask)
    return unpack(out)


def solution(mesh):
    in_specs = (
        P(("group", "tm"), None, None, None, None),
        P("group", None, None),
        P("group", None, None),
    )
    out_specs = P(("group", "tm"), None, None, None, None)
    return jax.shard_map(
        on_device, mesh=mesh, in_specs=in_specs, out_specs=out_specs, check_vma=False
    )
```

```python
import functools

import jax
import jax.numpy as jnp
from jax import lax
from jax.experimental import pallas as pl
from jax.experimental.pallas import tpu as pltpu
from jax.sharding import PartitionSpec as P

MSTEPS = 8
PULSE = 16
LANES = 128
ROWS = 8

time_step = 0.05
excite_gain = 8.0
threshold = 0.15
recovery_base = 0.005
recovery_gain = 0.2
recovery_shift = 0.3
pulse_height = 1.0
coarse_floor = -0.5
conduct_table = (0.1, 0.35, 0.7, 1.0)


def inverse(value):
    guess = pl.reciprocal(value, approx=True)
    return guess * (2.0 - value * guess)


def scaled_rate(potential, recovery, scale):
    above = (scale * recovery_gain) * jnp.maximum(recovery, 0.0)
    return scale * recovery_base + above * inverse(jnp.maximum(potential, 0.0) + recovery_shift)


def compose(earlier, latter):
    return (
        latter[0] * earlier[0],
        latter[1] * earlier[0] + latter[2] * earlier[1],
        latter[2] * earlier[2],
        latter[0] * earlier[3] + latter[3],
        latter[1] * earlier[3] + latter[2] * earlier[4] + latter[4],
    )


def apply_map(mapping, first_in, second_in):
    return (
        mapping[0] * first_in + mapping[3],
        mapping[1] * first_in + mapping[2] * second_in + mapping[4],
    )


def loop_point(loop_map):
    first_part = loop_map[3] / (1.0 - loop_map[0])
    second = (loop_map[4] + loop_map[1] * first_part) / (1.0 - loop_map[2])
    return (first_part, second)


def neighbours(ref, slot, tile, lane):
    here = pl.ds(ROWS + ROWS * tile, ROWS)
    above = pl.ds(ROWS - 1 + ROWS * tile, ROWS)
    below = pl.ds(ROWS + 1 + ROWS * tile, ROWS)
    mid = [ref[slot, k, here] for k in range(3)]
    up = [ref[slot, k, above] for k in range(3)]
    down = [ref[slot, k, below] for k in range(3)]
    first, second, rest = mid
    swapped = pltpu.roll(rest, 64, 1)
    first_left = pltpu.roll(first, 1, 1)
    rest_right = pltpu.roll(rest, LANES - 1, 1)
    left = [
        first_left,
        pltpu.roll(second, 1, 1),
        jnp.where(
            lane == 0,
            first_left,
            jnp.where(lane == 64, pltpu.roll(second, 65, 1), pltpu.roll(rest, 1, 1)),
        ),
    ]
    right = [
        jnp.where(lane == LANES - 1, rest_right, pltpu.roll(first, LANES - 1, 1)),
        jnp.where(
            lane == LANES - 1,
            pltpu.roll(swapped, LANES - 1, 1),
            pltpu.roll(second, LANES - 1, 1),
        ),
        rest_right,
    ]
    return mid, up, down, left, right, [second, first, swapped]


def packed(ref, place, here):
    first, second = ref[(*place, 0, here)], ref[(*place, 1, here)]
    rest = jnp.concatenate([first[:, LANES:], second[:, LANES:]], axis=1)
    return [first[:, :LANES], second[:, :LANES], rest]


def slot_map(prev_p, prev_q, relax_p, relax_q):
    potential = jnp.clip(prev_p, 0.0, 1.0)
    recovery = jnp.maximum(prev_q, 0.0)
    recover_rate = scaled_rate(potential, recovery, 1.0)
    horizon = MSTEPS * time_step
    fast_slope = jnp.minimum(
        -excite_gain
        * (3.0 * potential * potential - 2.0 * (1.0 + threshold) * potential + threshold)
        - recovery,
        coarse_floor,
    )
    cross_term = -recover_rate * excite_gain * (2.0 * potential - threshold - 1.0)
    first_diag = inverse(1.0 - horizon * fast_slope)
    second_diag = inverse(1.0 + horizon * recover_rate)
    lower_term = horizon * cross_term * first_diag * second_diag
    return (first_diag, lower_term, second_diag, prev_p - relax_p, prev_q - relax_q)


def kernel(
    loop_size, chips, groups,
    iterate_hbm, labels_hbm, stim_hbm, out_ref,
    raw, raw_labels, raw_stim, it_ref, stim_ref, load_sem,
    pot, rec, drive, cond, coef, relaxed, previous, sent, maps, own, got, early, pair,
    parts, total, totals, leave, enter, pass_on, entry,
    ring_s, ring_r, a_s, a_r, b_s, b_r, g_s, g_r, c_s, c_r, d_s, d_r,
):
    slots = it_ref.shape[0]
    tiles = stim_ref.shape[1] // ROWS
    last = slots - 1
    loads = [
        pltpu.make_async_copy(labels_hbm, raw_labels, load_sem.at[slots]),
        pltpu.make_async_copy(stim_hbm, raw_stim, load_sem.at[slots + 1]),
    ]
    for s in reversed(range(slots)):
        loads.append(pltpu.make_async_copy(iterate_hbm.at[s], raw.at[s], load_sem.at[s]))
    for load in loads:
        load.start()
    half = tiles // 2
    me = lax.axis_index("tm")
    core = lax.rem(me, 2)
    chip = lax.rem(me // 2, chips)
    group = me // (2 * chips)
    base = group * 2 * chips
    partner = me + 1 - 2 * core
    right = lax.rem(me + 1, loop_size)
    across = lax.rem(me + 2 * core - 1 + loop_size, loop_size)
    owner = jnp.logical_and(chip != 1, chip != chips - 2)
    my_tile = chip - (chip + chips - 1) // chips - (chip + 2) // chips

    barrier = pltpu.get_barrier_semaphore()

    def greet(device):
        pl.semaphore_signal(
            barrier, inc=1, device_id={"tm": device}, device_id_type=pl.DeviceIdType.MESH
        )

    greet(partner)
    greet(across)
    for hop in range(1, chips):
        greet(base + 2 * lax.rem(chip + hop, chips) + core)
    for hop in range(1, groups):
        greet(lax.rem(me + hop * 2 * chips, loop_size))

    def remote(source, target, send_sem, recv_sem, device):
        return pltpu.make_async_remote_copy(
            src_ref=source, dst_ref=target, send_sem=send_sem, recv_sem=recv_sem,
            device_id={"tm": device}, device_id_type=pl.DeviceIdType.MESH,
        )

    lane = lax.broadcasted_iota(jnp.int32, (ROWS, LANES), 1)
    row = lax.broadcasted_iota(jnp.int32, (ROWS, LANES), 0)
    edge = jnp.zeros((ROWS, LANES), jnp.float32)
    for k in range(3):
        for end in (0, ROWS + ROWS * tiles):
            cond[0, k, pl.ds(end, ROWS)] = edge
            pot[0, k, pl.ds(end, ROWS)] = edge
            pot[1, k, pl.ds(end, ROWS)] = edge
    loads[0].wait()
    for t in range(tiles):
        here = pl.ds(ROWS * t, ROWS)
        for k, label in enumerate(packed(raw_labels, (), here)):
            conduct = jnp.full((ROWS, LANES), conduct_table[0], jnp.float32)
            for label_id in range(1, len(conduct_table)):
                conduct = jnp.where(label == label_id, conduct_table[label_id], conduct)
            cond[0, k, pl.ds(ROWS + ROWS * t, ROWS)] = conduct
    loads[1].wait()
    for t in range(tiles):
        here = pl.ds(ROWS * t, ROWS)
        for k, mask in enumerate(packed(raw_stim, (), here)):
            stim_ref[k, here] = mask.astype(jnp.float32)
    for t in range(tiles):
        mid, up, down, left, right_, over = neighbours(cond, 0, t, lane)
        here = pl.ds(ROWS * t, ROWS)
        for k in range(3):
            def face(value, open_face=None):
                mean = time_step * 0.5 * (mid[k] + value)
                return mean if open_face is None else jnp.where(open_face, mean, 0.0)

            faces = (
                face(up[k], row > 0 if t == 0 else None),
                face(down[k], row < ROWS - 1 if t == tiles - 1 else None),
                face(left[k], lane > 0 if k < 2 else None),
                face(
                    right_[k],
                    None if k < 2 else jnp.logical_and(lane != 63, lane != LANES - 1),
                ),
                face(over[k]),
            )
            for n, value in enumerate(faces):
                coef[n, k, here] = value
            stay = 1.0 - time_step * excite_gain * threshold
            coef[5, k, here] = stay - (((faces[0] + faces[1]) + (faces[2] + faces[3])) + faces[4])

    def unload(s):
        loads[2 + last - s].wait()
        for n in range(2):
            for t in range(tiles):
                here = pl.ds(ROWS * t, ROWS)
                for k, value in enumerate(packed(raw, (s, n), here)):
                    it_ref[s, n, k, here] = value

    def advance(source, target, slice_index):
        switch = jnp.where(slice_index * MSTEPS < PULSE, time_step * pulse_height, 0.0)
        for k in range(3):
            pot[0, k, pl.ds(ROWS, ROWS * tiles)] = source[0, k]
            rec[k] = source[1, k]
            drive[k] = switch * stim_ref[k]

        def two_steps(turn, carry):
            for now in (0, 1):
                for t in range(tiles):
                    mid, up, down, left, right_, over = neighbours(pot, now, t, lane)
                    here = pl.ds(ROWS * t, ROWS)
                    for k in range(3):
                        p, q = mid[k], rec[k, here]
                        flow = coef[0, k, here] * up[k] + coef[1, k, here] * down[k]
                        flow = flow + (coef[2, k, here] * left[k] + coef[3, k, here] * right_[k])
                        flow = flow + (coef[4, k, here] * over[k] + drive[k, here])
                        pull = q + excite_gain * (p * (p - (threshold + 1.0)))
                        keep = coef[5, k, here] - time_step * pull
                        pot[1 - now, k, pl.ds(ROWS + ROWS * t, ROWS)] = p * keep + flow
                        rec[k, here] = q - scaled_rate(p, q, time_step) * pull
            return carry

        lax.fori_loop(0, MSTEPS // 2, two_steps, 0)
        for k in range(3):
            target[0, k] = pot[0, k, pl.ds(ROWS, ROWS * tiles)]
            target[1, k] = rec[k]

    first_slice = me * slots
    unload(last)
    advance(it_ref.at[last], sent.at[0], first_slice + last)
    pl.semaphore_wait(barrier, chips + 1 + groups - 1)
    ring_one = remote(sent.at[0], relaxed.at[0], ring_s.at[0], ring_r.at[0], right)
    ring_one.start()
    for s in reversed(range(last)):
        unload(s)
        advance(it_ref.at[s], relaxed.at[s + 1], first_slice + s)
    ring_two = remote(sent.at[1], previous.at[0], ring_s.at[1], ring_r.at[1], right)
    for s in reversed(range(slots)):
        if s == 0:
            ring_one.wait_recv()
        if s == last:
            advance(relaxed.at[s], sent.at[1], first_slice + s)
            ring_two.start()
        else:
            advance(relaxed.at[s], previous.at[s + 1], first_slice + s)
    ring_two.wait_recv()

    def make_maps(t):
        here = pl.ds(pl.multiple_of(ROWS * t, ROWS), ROWS)
        for k in range(3):
            whole = None
            for s in range(slots):
                mapping = slot_map(
                    previous[s, 0, k, here], previous[s, 1, k, here],
                    relaxed[s, 0, k, here], relaxed[s, 1, k, here],
                )
                for n in range(5):
                    maps[s, t, n, k] = mapping[n]
                whole = mapping if whole is None else compose(whole, mapping)
            for n in range(5):
                own[t, n, k] = whole[n]

    def fields(ref, *place):
        return tuple(ref[(*place, n)] for n in range(5))

    def a_copy(j):
        return remote(
            own.at[half * (1 - core) + j], got.at[j], a_s.at[j], a_r.at[j], partner
        )

    def phase_send(j, carry):
        make_maps(half * (1 - core) + j)
        a_copy(j).start()
        return carry

    def phase_keep(j, carry):
        make_maps(half * core + j)
        return carry

    lax.fori_loop(0, half, phase_send, 0)
    lax.fori_loop(0, half, phase_keep, 0)

    def owner_of(j):
        return j + (j + half - 1) // half + (j + 1) // half

    def b_copy(j):
        return remote(
            pair.at[j], parts.at[chip], b_s.at[j], b_r.at[chip],
            base + 2 * owner_of(j) + core,
        )

    def phase_pair(turn, carry):
        j = lax.rem(turn + chip, half)
        a_copy(j).wait_recv()
        for k in range(3):
            mine = tuple(own[half * core + j, n, k] for n in range(5))
            theirs = tuple(got[j, n, k] for n in range(5))
            is_first = core == 0
            earlier = tuple(jnp.where(is_first, m, h) for m, h in zip(mine, theirs))
            later = tuple(jnp.where(is_first, h, m) for m, h in zip(mine, theirs))
            both = compose(earlier, later)
            for n in range(5):
                early[j, n, k] = earlier[n]
                pair[j, n, k] = both[n]

        @pl.when(owner_of(j) != chip)
        def _():
            b_copy(j).start()

        @pl.when(owner_of(j) == chip)
        def _():
            parts[chip] = pair[j]

        return carry

    lax.fori_loop(0, half, phase_pair, 0)

    def c_copy(k):
        return remote(
            leave.at[k], enter.at[my_tile], c_s.at[k], c_r.at[my_tile], base + 2 * k + core
        )

    @pl.when(owner)
    def _():
        for k in range(chips):
            @pl.when(chip != k)
            def _():
                remote(
                    pair.at[0], parts.at[k], b_s.at[0], b_r.at[k], base + 2 * k + core
                ).wait_recv()

        whole = fields(parts, 0)
        for k in range(1, chips):
            whole = compose(whole, fields(parts, k))
        if groups == 1:
            state = loop_point(whole)
        else:
            total[...] = jnp.stack(whole)
            totals[group] = total[...]

            def g_copy(hop):
                to = lax.rem(me + hop * 2 * chips, loop_size)
                return remote(total, totals.at[group], g_s.at[hop], g_r.at[hop], to)

            for hop in range(1, groups):
                g_copy(hop).start()
            for hop in range(1, groups):
                g_copy(hop).wait()
            whole = fields(totals, 0)
            for g in range(1, groups):
                whole = compose(whole, fields(totals, g))
            state = loop_point(whole)
            for g in range(groups - 1):
                after = apply_map(fields(totals, g), state[0], state[1])
                state = tuple(jnp.where(g < group, n, o) for n, o in zip(after, state))
        for k in range(chips):
            leave[k, 0] = state[0]
            leave[k, 1] = state[1]

            @pl.when(chip != k)
            def _():
                c_copy(k).start()

            @pl.when(chip == k)
            def _():
                enter[my_tile] = leave[k]

            if k < chips - 1:
                state = apply_map(fields(parts, k), state[0], state[1])

    def finish(t):
        here = pl.ds(pl.multiple_of(ROWS * t, ROWS), ROWS)
        for k in range(3):
            value = (entry[t, 0, k], entry[t, 1, k])
            for s in range(slots):
                mapping = tuple(maps[s, t, n, k] for n in range(5))
                value = apply_map(mapping, value[0], value[1])
                out_ref[s, 0, k, here] = relaxed[s, 0, k, here] + value[0]
                out_ref[s, 1, k, here] = relaxed[s, 1, k, here] + value[1]

    def d_copy(j):
        return remote(pass_on.at[j], entry.at[half * core + j], d_s.at[j], d_r.at[j], partner)

    def phase_back(j, carry):
        @pl.when(owner_of(j) != chip)
        def _():
            remote(
                leave.at[0], enter.at[j], c_s.at[0], c_r.at[j], base + 2 * owner_of(j) + core
            ).wait_recv()

        for k in range(3):
            zero = (enter[j, 0, k], enter[j, 1, k])
            one = apply_map(tuple(early[j, n, k] for n in range(5)), zero[0], zero[1])
            for n in range(2):
                entry[half * core + j, n, k] = jnp.where(core == 0, zero[n], one[n])
                pass_on[j, n, k] = jnp.where(core == 0, one[n], zero[n])
        d_copy(j).start()
        return carry

    lax.fori_loop(0, half, phase_back, 0)

    def phase_mine(j, carry):
        finish(half * core + j)
        return carry

    def phase_theirs(j, carry):
        remote(
            pass_on.at[j], entry.at[half * (1 - core) + j], d_s.at[j], d_r.at[j], partner
        ).wait_recv()
        finish(half * (1 - core) + j)
        return carry

    lax.fori_loop(0, half, phase_mine, 0)
    lax.fori_loop(0, half, phase_theirs, 0)

    ring_one.wait_send()
    ring_two.wait_send()
    for j in range(half):
        a_copy(j).wait_send()
        d_copy(j).wait_send()

        @pl.when(owner_of(j) != chip)
        def _():
            b_copy(j).wait_send()

    @pl.when(owner)
    def _():
        for k in range(chips):
            @pl.when(chip != k)
            def _():
                c_copy(k).wait_send()


def unpack(packed):
    rest = packed[..., 2, :, :]
    rest = jnp.stack([rest[..., : LANES // 2], rest[..., LANES // 2 :]], axis=-3)
    return jnp.concatenate([packed[..., :2, :, :], rest], axis=-1)


def on_device(iterate, labels, stim_mask):
    loop_size = lax.axis_size("tm")
    chips = 8
    groups = loop_size // (2 * chips)
    slots = iterate.shape[0]
    rows = labels.shape[1]
    tiles = rows // ROWS
    half = tiles // 2
    f32 = jnp.float32
    state = (slots, 2, 3, rows, LANES)
    block = (3, ROWS, LANES)
    dma = pltpu.SemaphoreType.DMA
    out = pl.pallas_call(
        functools.partial(kernel, loop_size, chips, groups),
        out_shape=jax.ShapeDtypeStruct(state, f32),
        in_specs=[pl.BlockSpec(memory_space=pl.ANY)] * 3,
        out_specs=pl.BlockSpec(memory_space=pltpu.VMEM),
        scratch_shapes=[
            pltpu.VMEM(iterate.shape, f32),
            pltpu.VMEM(labels.shape, labels.dtype),
            pltpu.VMEM(stim_mask.shape, stim_mask.dtype),
            pltpu.VMEM(state, f32),
            pltpu.VMEM((3, rows, LANES), f32),
            pltpu.SemaphoreType.DMA((slots + 2,)),
            pltpu.VMEM((2, 3, rows + 2 * ROWS, LANES), f32),
            pltpu.VMEM((3, rows, LANES), f32),
            pltpu.VMEM((3, rows, LANES), f32),
            pltpu.VMEM((1, 3, rows + 2 * ROWS, LANES), f32),
            pltpu.VMEM((6, 3, rows, LANES), f32),
            pltpu.VMEM(state, f32),
            pltpu.VMEM(state, f32),
            pltpu.VMEM((2, 2, 3, rows, LANES), f32),
            pltpu.VMEM((slots, tiles, 5) + block, f32),
            pltpu.VMEM((tiles, 5) + block, f32),
            pltpu.VMEM((half, 5) + block, f32),
            pltpu.VMEM((half, 5) + block, f32),
            pltpu.VMEM((half, 5) + block, f32),
            pltpu.VMEM((chips, 5) + block, f32),
            pltpu.VMEM((5,) + block, f32),
            pltpu.VMEM((groups, 5) + block, f32),
            pltpu.VMEM((chips, 2) + block, f32),
            pltpu.VMEM((half, 2) + block, f32),
            pltpu.VMEM((half, 2) + block, f32),
            pltpu.VMEM((tiles, 2) + block, f32),
            dma((2,)), dma((2,)),
            dma((half,)), dma((half,)),
            dma((half,)), dma((chips,)),
            dma((groups,)), dma((groups,)),
            dma((chips,)), dma((half,)),
            dma((half,)), dma((half,)),
        ],
        compiler_params=pltpu.CompilerParams(
            collective_id=0, has_side_effects=True, vmem_limit_bytes=32 * 1024 * 1024
        ),
    )(iterate, labels, stim_mask)
    return unpack(out)


def solution(mesh):
    in_specs = (
        P(("group", "tm"), None, None, None, None),
        P("group", None, None),
        P("group", None, None),
    )
    out_specs = P(("group", "tm"), None, None, None, None)
    return jax.shard_map(
        on_device, mesh=mesh, in_specs=in_specs, out_specs=out_specs, check_vma=False
    )
```

```python
import functools

import jax
import jax.numpy as jnp
from jax import lax
from jax.experimental import pallas as pl
from jax.experimental.pallas import tpu as pltpu
from jax.sharding import PartitionSpec as P

MSTEPS = 8
PULSE = 16
LANES = 128
ROWS = 8

time_step = 0.05
excite_gain = 8.0
threshold = 0.15
recovery_base = 0.005
recovery_gain = 0.2
recovery_shift = 0.3
pulse_height = 1.0
coarse_floor = -0.5
conduct_table = (0.1, 0.35, 0.7, 1.0)


def inverse(value):
    guess = pl.reciprocal(value, approx=True)
    return guess * (2.0 - value * guess)


def scaled_rate(potential, recovery, scale):
    above = (scale * recovery_gain) * jnp.maximum(recovery, 0.0)
    return scale * recovery_base + above * inverse(jnp.maximum(potential, 0.0) + recovery_shift)


def compose(earlier, latter):
    return (
        latter[0] * earlier[0],
        latter[1] * earlier[0] + latter[2] * earlier[1],
        latter[2] * earlier[2],
        latter[0] * earlier[3] + latter[3],
        latter[1] * earlier[3] + latter[2] * earlier[4] + latter[4],
    )


def apply_map(mapping, first_in, second_in):
    return (
        mapping[0] * first_in + mapping[3],
        mapping[1] * first_in + mapping[2] * second_in + mapping[4],
    )


def loop_point(loop_map):
    first_part = loop_map[3] / (1.0 - loop_map[0])
    second = (loop_map[4] + loop_map[1] * first_part) / (1.0 - loop_map[2])
    return (first_part, second)


def neighbours(ref, slot, tile, lane):
    here = pl.ds(ROWS + ROWS * tile, ROWS)
    above = pl.ds(ROWS - 1 + ROWS * tile, ROWS)
    below = pl.ds(ROWS + 1 + ROWS * tile, ROWS)
    mid = [ref[slot, k, here] for k in range(3)]
    up = [ref[slot, k, above] for k in range(3)]
    down = [ref[slot, k, below] for k in range(3)]
    first, second, rest = mid
    swapped = pltpu.roll(rest, 64, 1)
    first_left = pltpu.roll(first, 1, 1)
    rest_right = pltpu.roll(rest, LANES - 1, 1)
    left = [
        first_left,
        pltpu.roll(second, 1, 1),
        jnp.where(
            lane == 0,
            first_left,
            jnp.where(lane == 64, pltpu.roll(second, 65, 1), pltpu.roll(rest, 1, 1)),
        ),
    ]
    right = [
        jnp.where(lane == LANES - 1, rest_right, pltpu.roll(first, LANES - 1, 1)),
        jnp.where(
            lane == LANES - 1,
            pltpu.roll(swapped, LANES - 1, 1),
            pltpu.roll(second, LANES - 1, 1),
        ),
        rest_right,
    ]
    return mid, up, down, left, right, [second, first, swapped]


def packed(ref, place, here):
    first, second = ref[(*place, 0, here)], ref[(*place, 1, here)]
    rest = jnp.concatenate([first[:, LANES:], second[:, LANES:]], axis=1)
    return [first[:, :LANES], second[:, :LANES], rest]


def slot_map(prev_p, prev_q, relax_p, relax_q):
    potential = jnp.clip(prev_p, 0.0, 1.0)
    recovery = jnp.maximum(prev_q, 0.0)
    recover_rate = scaled_rate(potential, recovery, 1.0)
    horizon = MSTEPS * time_step
    fast_slope = jnp.minimum(
        -excite_gain
        * (3.0 * potential * potential - 2.0 * (1.0 + threshold) * potential + threshold)
        - recovery,
        coarse_floor,
    )
    cross_term = -recover_rate * excite_gain * (2.0 * potential - threshold - 1.0)
    first_diag = inverse(1.0 - horizon * fast_slope)
    second_diag = inverse(1.0 + horizon * recover_rate)
    lower_term = horizon * cross_term * first_diag * second_diag
    return (first_diag, lower_term, second_diag, prev_p - relax_p, prev_q - relax_q)


def kernel(
    loop_size, chips, groups,
    iterate_hbm, labels_hbm, stim_hbm, out_ref,
    raw, raw_labels, raw_stim, it_ref, stim_ref, load_sem,
    pot, rec, drive, cond, coef, relaxed, previous, sent, maps, own, got, early, pair,
    parts, total, totals, leave, enter, pass_on, entry,
    ring_s, ring_r, a_s, a_r, b_s, b_r, g_s, g_r, c_s, c_r, d_s, d_r,
):
    slots = it_ref.shape[0]
    tiles = stim_ref.shape[1] // ROWS
    last = slots - 1
    loads = [
        pltpu.make_async_copy(labels_hbm, raw_labels, load_sem.at[slots]),
        pltpu.make_async_copy(stim_hbm, raw_stim, load_sem.at[slots + 1]),
    ]
    for s in reversed(range(slots)):
        loads.append(pltpu.make_async_copy(iterate_hbm.at[s], raw.at[s], load_sem.at[s]))
    for load in loads:
        load.start()
    half = tiles // 2
    me = lax.axis_index("tm")
    core = lax.rem(me, 2)
    chip = lax.rem(me // 2, chips)
    group = me // (2 * chips)
    base = group * 2 * chips
    partner = me + 1 - 2 * core
    right = lax.rem(me + 1, loop_size)
    across = lax.rem(me + 2 * core - 1 + loop_size, loop_size)
    owner = jnp.logical_and(chip != 1, chip != chips - 2)
    my_tile = chip - (chip + chips - 1) // chips - (chip + 2) // chips

    barrier = pltpu.get_barrier_semaphore()

    def greet(device):
        pl.semaphore_signal(
            barrier, inc=1, device_id={"tm": device}, device_id_type=pl.DeviceIdType.MESH
        )

    greet(partner)
    greet(across)
    for hop in range(1, chips):
        greet(base + 2 * lax.rem(chip + hop, chips) + core)
    for hop in range(1, groups):
        greet(lax.rem(me + hop * 2 * chips, loop_size))

    def remote(source, target, send_sem, recv_sem, device):
        return pltpu.make_async_remote_copy(
            src_ref=source, dst_ref=target, send_sem=send_sem, recv_sem=recv_sem,
            device_id={"tm": device}, device_id_type=pl.DeviceIdType.MESH,
        )

    lane = lax.broadcasted_iota(jnp.int32, (ROWS, LANES), 1)
    row = lax.broadcasted_iota(jnp.int32, (ROWS, LANES), 0)
    edge = jnp.zeros((ROWS, LANES), jnp.float32)
    for k in range(3):
        for end in (0, ROWS + ROWS * tiles):
            cond[0, k, pl.ds(end, ROWS)] = edge
            pot[0, k, pl.ds(end, ROWS)] = edge
            pot[1, k, pl.ds(end, ROWS)] = edge
    loads[0].wait()
    for t in range(tiles):
        here = pl.ds(ROWS * t, ROWS)
        for k, label in enumerate(packed(raw_labels, (), here)):
            conduct = jnp.full((ROWS, LANES), conduct_table[0], jnp.float32)
            for label_id in range(1, len(conduct_table)):
                conduct = jnp.where(label == label_id, conduct_table[label_id], conduct)
            cond[0, k, pl.ds(ROWS + ROWS * t, ROWS)] = conduct
    loads[1].wait()
    for t in range(tiles):
        here = pl.ds(ROWS * t, ROWS)
        for k, mask in enumerate(packed(raw_stim, (), here)):
            stim_ref[k, here] = mask.astype(jnp.float32)
    for t in range(tiles):
        mid, up, down, left, right_, over = neighbours(cond, 0, t, lane)
        here = pl.ds(ROWS * t, ROWS)
        for k in range(3):
            def face(value, open_face=None):
                mean = time_step * 0.5 * (mid[k] + value)
                return mean if open_face is None else jnp.where(open_face, mean, 0.0)

            faces = (
                face(up[k], row > 0 if t == 0 else None),
                face(down[k], row < ROWS - 1 if t == tiles - 1 else None),
                face(left[k], lane > 0 if k < 2 else None),
                face(
                    right_[k],
                    None if k < 2 else jnp.logical_and(lane != 63, lane != LANES - 1),
                ),
                face(over[k]),
            )
            for n, value in enumerate(faces):
                coef[n, k, here] = value
            stay = 1.0 - time_step * excite_gain * threshold
            coef[5, k, here] = stay - (((faces[0] + faces[1]) + (faces[2] + faces[3])) + faces[4])

    def unload(s):
        loads[2 + last - s].wait()
        for n in range(2):
            for t in range(tiles):
                here = pl.ds(ROWS * t, ROWS)
                for k, value in enumerate(packed(raw, (s, n), here)):
                    it_ref[s, n, k, here] = value

    def advance(source, target, slice_index):
        switch = jnp.where(slice_index * MSTEPS < PULSE, time_step * pulse_height, 0.0)
        for k in range(3):
            pot[0, k, pl.ds(ROWS, ROWS * tiles)] = source[0, k]
            rec[k] = source[1, k]
            drive[k] = switch * stim_ref[k]

        def two_steps(turn, carry):
            for now in (0, 1):
                for t in range(tiles):
                    mid, up, down, left, right_, over = neighbours(pot, now, t, lane)
                    here = pl.ds(ROWS * t, ROWS)
                    for k in range(3):
                        p, q = mid[k], rec[k, here]
                        flow = coef[0, k, here] * up[k] + coef[1, k, here] * down[k]
                        flow = flow + (coef[2, k, here] * left[k] + coef[3, k, here] * right_[k])
                        flow = flow + (coef[4, k, here] * over[k] + drive[k, here])
                        pull = q + excite_gain * (p * (p - (threshold + 1.0)))
                        keep = coef[5, k, here] - time_step * pull
                        pot[1 - now, k, pl.ds(ROWS + ROWS * t, ROWS)] = p * keep + flow
                        rec[k, here] = q - scaled_rate(p, q, time_step) * pull
            return carry

        lax.fori_loop(0, MSTEPS // 2, two_steps, 0)
        for k in range(3):
            target[0, k] = pot[0, k, pl.ds(ROWS, ROWS * tiles)]
            target[1, k] = rec[k]

    first_slice = me * slots
    unload(last)
    advance(it_ref.at[last], sent.at[0], first_slice + last)
    pl.semaphore_wait(barrier, chips + 1 + groups - 1)
    ring_one = remote(sent.at[0], relaxed.at[0], ring_s.at[0], ring_r.at[0], right)
    ring_one.start()
    for s in reversed(range(last)):
        unload(s)
        advance(it_ref.at[s], relaxed.at[s + 1], first_slice + s)

    def ring_two(t):
        here = pl.ds(pl.multiple_of(ROWS * t, ROWS), ROWS)
        return remote(
            sent.at[1, :, :, here], previous.at[0, :, :, here],
            ring_s.at[1 + t], ring_r.at[1 + t], right,
        )

    def send_two(turn, carry):
        j = lax.rem(turn + lax.rem(right // 2, chips), half)
        ring_two(half * core + j).start()
        ring_two(half * (1 - core) + j).start()
        return carry

    for s in reversed(range(slots)):
        if s == 0:
            ring_one.wait_recv()
        if s == last:
            advance(relaxed.at[s], sent.at[1], first_slice + s)
            lax.fori_loop(0, half, send_two, 0)
        else:
            advance(relaxed.at[s], previous.at[s + 1], first_slice + s)

    def make_maps(t):
        here = pl.ds(pl.multiple_of(ROWS * t, ROWS), ROWS)
        for k in range(3):
            whole = None
            for s in range(slots):
                mapping = slot_map(
                    previous[s, 0, k, here], previous[s, 1, k, here],
                    relaxed[s, 0, k, here], relaxed[s, 1, k, here],
                )
                for n in range(5):
                    maps[s, t, n, k] = mapping[n]
                whole = mapping if whole is None else compose(whole, mapping)
            for n in range(5):
                own[t, n, k] = whole[n]

    def fields(ref, *place):
        return tuple(ref[(*place, n)] for n in range(5))

    def a_copy(j):
        return remote(
            own.at[half * (1 - core) + j], got.at[j], a_s.at[j], a_r.at[j], partner
        )

    def owner_of(j):
        return j + (j + half - 1) // half + (j + 1) // half

    def b_copy(j):
        return remote(
            pair.at[j], parts.at[chip], b_s.at[j], b_r.at[chip],
            base + 2 * owner_of(j) + core,
        )

    def pair_step(turn):
        j = lax.rem(turn + chip, half)
        a_copy(j).wait_recv()
        for k in range(3):
            mine = tuple(own[half * core + j, n, k] for n in range(5))
            theirs = tuple(got[j, n, k] for n in range(5))
            is_first = core == 0
            earlier = tuple(jnp.where(is_first, m, h) for m, h in zip(mine, theirs))
            later = tuple(jnp.where(is_first, h, m) for m, h in zip(mine, theirs))
            both = compose(earlier, later)
            for n in range(5):
                early[j, n, k] = earlier[n]
                pair[j, n, k] = both[n]

        @pl.when(owner_of(j) != chip)
        def _():
            b_copy(j).start()

        @pl.when(owner_of(j) == chip)
        def _():
            parts[chip] = pair[j]

    def phase_maps(turn, carry):
        j = lax.rem(turn + chip, half)
        away, mine = half * (1 - core) + j, half * core + j
        ring_two(away).wait_recv()
        make_maps(away)
        a_copy(j).start()
        ring_two(mine).wait_recv()
        make_maps(mine)

        @pl.when(turn > 0)
        def _():
            pair_step(turn - 1)

        return carry

    lax.fori_loop(0, half, phase_maps, 0)
    pair_step(half - 1)

    def c_copy(k):
        return remote(
            leave.at[k], enter.at[my_tile], c_s.at[k], c_r.at[my_tile], base + 2 * k + core
        )

    @pl.when(owner)
    def _():
        for k in range(chips):
            @pl.when(chip != k)
            def _():
                remote(
                    pair.at[0], parts.at[k], b_s.at[0], b_r.at[k], base + 2 * k + core
                ).wait_recv()

        whole = fields(parts, 0)
        for k in range(1, chips):
            whole = compose(whole, fields(parts, k))
        if groups == 1:
            state = loop_point(whole)
        else:
            total[...] = jnp.stack(whole)
            totals[group] = total[...]

            def g_copy(hop):
                to = lax.rem(me + hop * 2 * chips, loop_size)
                return remote(total, totals.at[group], g_s.at[hop], g_r.at[hop], to)

            for hop in range(1, groups):
                g_copy(hop).start()
            for hop in range(1, groups):
                g_copy(hop).wait()
            whole = fields(totals, 0)
            for g in range(1, groups):
                whole = compose(whole, fields(totals, g))
            state = loop_point(whole)
            for g in range(groups - 1):
                after = apply_map(fields(totals, g), state[0], state[1])
                state = tuple(jnp.where(g < group, n, o) for n, o in zip(after, state))
        for k in range(chips):
            leave[k, 0] = state[0]
            leave[k, 1] = state[1]

            @pl.when(chip != k)
            def _():
                c_copy(k).start()

            @pl.when(chip == k)
            def _():
                enter[my_tile] = leave[k]

            if k < chips - 1:
                state = apply_map(fields(parts, k), state[0], state[1])

    def finish(t):
        here = pl.ds(pl.multiple_of(ROWS * t, ROWS), ROWS)
        for k in range(3):
            value = (entry[t, 0, k], entry[t, 1, k])
            for s in range(slots):
                mapping = tuple(maps[s, t, n, k] for n in range(5))
                value = apply_map(mapping, value[0], value[1])
                out_ref[s, 0, k, here] = relaxed[s, 0, k, here] + value[0]
                out_ref[s, 1, k, here] = relaxed[s, 1, k, here] + value[1]

    def d_copy(j):
        return remote(pass_on.at[j], entry.at[half * core + j], d_s.at[j], d_r.at[j], partner)

    def phase_back(j, carry):
        @pl.when(owner_of(j) != chip)
        def _():
            remote(
                leave.at[0], enter.at[j], c_s.at[0], c_r.at[j], base + 2 * owner_of(j) + core
            ).wait_recv()

        for k in range(3):
            zero = (enter[j, 0, k], enter[j, 1, k])
            one = apply_map(tuple(early[j, n, k] for n in range(5)), zero[0], zero[1])
            for n in range(2):
                entry[half * core + j, n, k] = jnp.where(core == 0, zero[n], one[n])
                pass_on[j, n, k] = jnp.where(core == 0, one[n], zero[n])
        d_copy(j).start()
        return carry

    lax.fori_loop(0, half, phase_back, 0)

    def phase_mine(j, carry):
        finish(half * core + j)
        return carry

    def phase_theirs(j, carry):
        remote(
            pass_on.at[j], entry.at[half * (1 - core) + j], d_s.at[j], d_r.at[j], partner
        ).wait_recv()
        finish(half * (1 - core) + j)
        return carry

    lax.fori_loop(0, half, phase_mine, 0)
    lax.fori_loop(0, half, phase_theirs, 0)

    ring_one.wait_send()
    for t in range(tiles):
        ring_two(t).wait_send()
    for j in range(half):
        a_copy(j).wait_send()
        d_copy(j).wait_send()

        @pl.when(owner_of(j) != chip)
        def _():
            b_copy(j).wait_send()

    @pl.when(owner)
    def _():
        for k in range(chips):
            @pl.when(chip != k)
            def _():
                c_copy(k).wait_send()


def unpack(packed):
    rest = packed[..., 2, :, :]
    rest = jnp.stack([rest[..., : LANES // 2], rest[..., LANES // 2 :]], axis=-3)
    return jnp.concatenate([packed[..., :2, :, :], rest], axis=-1)


def on_device(iterate, labels, stim_mask):
    loop_size = lax.axis_size("tm")
    chips = 8
    groups = loop_size // (2 * chips)
    slots = iterate.shape[0]
    rows = labels.shape[1]
    tiles = rows // ROWS
    half = tiles // 2
    f32 = jnp.float32
    state = (slots, 2, 3, rows, LANES)
    block = (3, ROWS, LANES)
    dma = pltpu.SemaphoreType.DMA
    out = pl.pallas_call(
        functools.partial(kernel, loop_size, chips, groups),
        out_shape=jax.ShapeDtypeStruct(state, f32),
        in_specs=[pl.BlockSpec(memory_space=pl.ANY)] * 3,
        out_specs=pl.BlockSpec(memory_space=pltpu.VMEM),
        scratch_shapes=[
            pltpu.VMEM(iterate.shape, f32),
            pltpu.VMEM(labels.shape, labels.dtype),
            pltpu.VMEM(stim_mask.shape, stim_mask.dtype),
            pltpu.VMEM(state, f32),
            pltpu.VMEM((3, rows, LANES), f32),
            pltpu.SemaphoreType.DMA((slots + 2,)),
            pltpu.VMEM((2, 3, rows + 2 * ROWS, LANES), f32),
            pltpu.VMEM((3, rows, LANES), f32),
            pltpu.VMEM((3, rows, LANES), f32),
            pltpu.VMEM((1, 3, rows + 2 * ROWS, LANES), f32),
            pltpu.VMEM((6, 3, rows, LANES), f32),
            pltpu.VMEM(state, f32),
            pltpu.VMEM(state, f32),
            pltpu.VMEM((2, 2, 3, rows, LANES), f32),
            pltpu.VMEM((slots, tiles, 5) + block, f32),
            pltpu.VMEM((tiles, 5) + block, f32),
            pltpu.VMEM((half, 5) + block, f32),
            pltpu.VMEM((half, 5) + block, f32),
            pltpu.VMEM((half, 5) + block, f32),
            pltpu.VMEM((chips, 5) + block, f32),
            pltpu.VMEM((5,) + block, f32),
            pltpu.VMEM((groups, 5) + block, f32),
            pltpu.VMEM((chips, 2) + block, f32),
            pltpu.VMEM((half, 2) + block, f32),
            pltpu.VMEM((half, 2) + block, f32),
            pltpu.VMEM((tiles, 2) + block, f32),
            dma((1 + tiles,)), dma((1 + tiles,)),
            dma((half,)), dma((half,)),
            dma((half,)), dma((chips,)),
            dma((groups,)), dma((groups,)),
            dma((chips,)), dma((half,)),
            dma((half,)), dma((half,)),
        ],
        compiler_params=pltpu.CompilerParams(
            collective_id=0, has_side_effects=True, vmem_limit_bytes=32 * 1024 * 1024
        ),
    )(iterate, labels, stim_mask)
    return unpack(out)


def solution(mesh):
    in_specs = (
        P(("group", "tm"), None, None, None, None),
        P("group", None, None),
        P("group", None, None),
    )
    out_specs = P(("group", "tm"), None, None, None, None)
    return jax.shard_map(
        on_device, mesh=mesh, in_specs=in_specs, out_specs=out_specs, check_vma=False
    )
```

```python
import functools

import jax
import jax.numpy as jnp
from jax import lax
from jax.experimental import pallas as pl
from jax.experimental.pallas import tpu as pltpu
from jax.sharding import PartitionSpec as P

MSTEPS = 8
PULSE = 16
LANES = 128
ROWS = 8

time_step = 0.05
excite_gain = 8.0
threshold = 0.15
recovery_base = 0.005
recovery_gain = 0.2
recovery_shift = 0.3
pulse_height = 1.0
coarse_floor = -0.5
conduct_table = (0.1, 0.35, 0.7, 1.0)


def inverse(value):
    guess = pl.reciprocal(value, approx=True)
    return guess * (2.0 - value * guess)


def scaled_rate(potential, recovery, scale):
    above = (scale * recovery_gain) * jnp.maximum(recovery, 0.0)
    return scale * recovery_base + above * inverse(jnp.maximum(potential, 0.0) + recovery_shift)


def compose(earlier, latter):
    return (
        latter[0] * earlier[0],
        latter[1] * earlier[0] + latter[2] * earlier[1],
        latter[2] * earlier[2],
        latter[0] * earlier[3] + latter[3],
        latter[1] * earlier[3] + latter[2] * earlier[4] + latter[4],
    )


def apply_map(mapping, first_in, second_in):
    return (
        mapping[0] * first_in + mapping[3],
        mapping[1] * first_in + mapping[2] * second_in + mapping[4],
    )


def loop_point(loop_map):
    first_part = loop_map[3] / (1.0 - loop_map[0])
    second = (loop_map[4] + loop_map[1] * first_part) / (1.0 - loop_map[2])
    return (first_part, second)


def neighbours(ref, slot, tile, lane):
    here = pl.ds(ROWS + ROWS * tile, ROWS)
    above = pl.ds(ROWS - 1 + ROWS * tile, ROWS)
    below = pl.ds(ROWS + 1 + ROWS * tile, ROWS)
    mid = [ref[slot, k, here] for k in range(3)]
    up = [ref[slot, k, above] for k in range(3)]
    down = [ref[slot, k, below] for k in range(3)]
    first, second, rest = mid
    swapped = pltpu.roll(rest, 64, 1)
    first_left = pltpu.roll(first, 1, 1)
    rest_right = pltpu.roll(rest, LANES - 1, 1)
    left = [
        first_left,
        pltpu.roll(second, 1, 1),
        jnp.where(
            lane == 0,
            first_left,
            jnp.where(lane == 64, pltpu.roll(second, 65, 1), pltpu.roll(rest, 1, 1)),
        ),
    ]
    right = [
        jnp.where(lane == LANES - 1, rest_right, pltpu.roll(first, LANES - 1, 1)),
        jnp.where(
            lane == LANES - 1,
            pltpu.roll(swapped, LANES - 1, 1),
            pltpu.roll(second, LANES - 1, 1),
        ),
        rest_right,
    ]
    return mid, up, down, left, right, [second, first, swapped]


def packed(ref, place, here):
    first, second = ref[(*place, 0, here)], ref[(*place, 1, here)]
    rest = jnp.concatenate([first[:, LANES:], second[:, LANES:]], axis=1)
    return [first[:, :LANES], second[:, :LANES], rest]


def slot_map(prev_p, prev_q, relax_p, relax_q):
    potential = jnp.clip(prev_p, 0.0, 1.0)
    recovery = jnp.maximum(prev_q, 0.0)
    recover_rate = scaled_rate(potential, recovery, 1.0)
    horizon = MSTEPS * time_step
    fast_slope = jnp.minimum(
        -excite_gain
        * (3.0 * potential * potential - 2.0 * (1.0 + threshold) * potential + threshold)
        - recovery,
        coarse_floor,
    )
    cross_term = -recover_rate * excite_gain * (2.0 * potential - threshold - 1.0)
    first_diag = inverse(1.0 - horizon * fast_slope)
    second_diag = inverse(1.0 + horizon * recover_rate)
    lower_term = horizon * cross_term * first_diag * second_diag
    return (first_diag, lower_term, second_diag, prev_p - relax_p, prev_q - relax_q)


def kernel(
    loop_size, chips, groups,
    iterate_hbm, labels_hbm, stim_hbm, out_ref,
    raw, raw_labels, raw_stim, it_ref, stim_ref, load_sem,
    pot, rec, drive, cond, coef, relaxed, previous, sent, maps, own, got, early, pair,
    parts, total, totals, leave, enter, pass_on, entry,
    ring_s, ring_r, a_s, a_r, b_s, b_r, g_s, g_r, c_s, c_r, d_s, d_r,
):
    slots = it_ref.shape[0]
    tiles = stim_ref.shape[1] // ROWS
    last = slots - 1
    loads = [
        pltpu.make_async_copy(labels_hbm, raw_labels, load_sem.at[slots]),
        pltpu.make_async_copy(stim_hbm, raw_stim, load_sem.at[slots + 1]),
    ]
    for s in reversed(range(slots)):
        loads.append(pltpu.make_async_copy(iterate_hbm.at[s], raw.at[s], load_sem.at[s]))
    half = tiles // 2
    me = lax.axis_index("tm")
    core = lax.rem(me, 2)
    chip = lax.rem(me // 2, chips)
    group = me // (2 * chips)
    base = group * 2 * chips
    partner = me + 1 - 2 * core
    right = lax.rem(me + 1, loop_size)
    across = lax.rem(me + 2 * core - 1 + loop_size, loop_size)
    owner = jnp.logical_and(chip != 1, chip != chips - 2)
    my_tile = chip - (chip + chips - 1) // chips - (chip + 2) // chips

    barrier = pltpu.get_barrier_semaphore()

    def greet(device):
        pl.semaphore_signal(
            barrier, inc=1, device_id={"tm": device}, device_id_type=pl.DeviceIdType.MESH
        )

    greet(partner)
    greet(across)
    for hop in range(1, chips):
        greet(base + 2 * lax.rem(chip + hop, chips) + core)
    for hop in range(1, groups):
        greet(lax.rem(me + hop * 2 * chips, loop_size))

    def remote(source, target, send_sem, recv_sem, device):
        return pltpu.make_async_remote_copy(
            src_ref=source, dst_ref=target, send_sem=send_sem, recv_sem=recv_sem,
            device_id={"tm": device}, device_id_type=pl.DeviceIdType.MESH,
        )

    for load in loads:
        load.start()

    lane = lax.broadcasted_iota(jnp.int32, (ROWS, LANES), 1)
    row = lax.broadcasted_iota(jnp.int32, (ROWS, LANES), 0)
    edge = jnp.zeros((ROWS, LANES), jnp.float32)
    for k in range(3):
        for end in (0, ROWS + ROWS * tiles):
            cond[0, k, pl.ds(end, ROWS)] = edge
            pot[0, k, pl.ds(end, ROWS)] = edge
            pot[1, k, pl.ds(end, ROWS)] = edge
    loads[0].wait()
    for t in range(tiles):
        here = pl.ds(ROWS * t, ROWS)
        for k, label in enumerate(packed(raw_labels, (), here)):
            conduct = jnp.full((ROWS, LANES), conduct_table[0], jnp.float32)
            for label_id in range(1, len(conduct_table)):
                conduct = jnp.where(label == label_id, conduct_table[label_id], conduct)
            cond[0, k, pl.ds(ROWS + ROWS * t, ROWS)] = conduct
    loads[1].wait()
    for t in range(tiles):
        here = pl.ds(ROWS * t, ROWS)
        for k, mask in enumerate(packed(raw_stim, (), here)):
            stim_ref[k, here] = mask.astype(jnp.float32)
    for t in range(tiles):
        mid, up, down, left, right_, over = neighbours(cond, 0, t, lane)
        here = pl.ds(ROWS * t, ROWS)
        for k in range(3):
            def face(value, open_face=None):
                mean = time_step * 0.5 * (mid[k] + value)
                return mean if open_face is None else jnp.where(open_face, mean, 0.0)

            faces = (
                face(up[k], row > 0 if t == 0 else None),
                face(down[k], row < ROWS - 1 if t == tiles - 1 else None),
                face(left[k], lane > 0 if k < 2 else None),
                face(
                    right_[k],
                    None if k < 2 else jnp.logical_and(lane != 63, lane != LANES - 1),
                ),
                face(over[k]),
            )
            for n, value in enumerate(faces):
                coef[n, k, here] = value
            stay = 1.0 - time_step * excite_gain * threshold
            coef[5, k, here] = stay - (((faces[0] + faces[1]) + (faces[2] + faces[3])) + faces[4])

    def unload(s):
        loads[2 + last - s].wait()
        for n in range(2):
            for t in range(tiles):
                here = pl.ds(ROWS * t, ROWS)
                for k, value in enumerate(packed(raw, (s, n), here)):
                    it_ref[s, n, k, here] = value

    def advance(source, target, slice_index):
        switch = jnp.where(slice_index * MSTEPS < PULSE, time_step * pulse_height, 0.0)
        for k in range(3):
            pot[0, k, pl.ds(ROWS, ROWS * tiles)] = source[0, k]
            rec[k] = source[1, k]
            drive[k] = switch * stim_ref[k]

        def two_steps(turn, carry):
            for now in (0, 1):
                for t in range(tiles):
                    mid, up, down, left, right_, over = neighbours(pot, now, t, lane)
                    here = pl.ds(ROWS * t, ROWS)
                    for k in range(3):
                        p, q = mid[k], rec[k, here]
                        flow = coef[0, k, here] * up[k] + coef[1, k, here] * down[k]
                        flow = flow + (coef[2, k, here] * left[k] + coef[3, k, here] * right_[k])
                        flow = flow + (coef[4, k, here] * over[k] + drive[k, here])
                        pull = q + excite_gain * (p * (p - (threshold + 1.0)))
                        keep = coef[5, k, here] - time_step * pull
                        pot[1 - now, k, pl.ds(ROWS + ROWS * t, ROWS)] = p * keep + flow
                        rec[k, here] = q - scaled_rate(p, q, time_step) * pull
            return carry

        lax.fori_loop(0, MSTEPS // 2, two_steps, 0)
        for k in range(3):
            target[0, k] = pot[0, k, pl.ds(ROWS, ROWS * tiles)]
            target[1, k] = rec[k]

    first_slice = me * slots
    unload(last)
    advance(it_ref.at[last], sent.at[0], first_slice + last)
    pl.semaphore_wait(barrier, chips + 1 + groups - 1)
    ring_one = remote(sent.at[0], relaxed.at[0], ring_s.at[0], ring_r.at[0], right)
    ring_one.start()
    for s in reversed(range(last)):
        unload(s)
        advance(it_ref.at[s], relaxed.at[s + 1], first_slice + s)

    def ring_two(t):
        here = pl.ds(pl.multiple_of(ROWS * t, ROWS), ROWS)
        return remote(
            sent.at[1, :, :, here], previous.at[0, :, :, here],
            ring_s.at[1 + t], ring_r.at[1 + t], right,
        )

    def send_two(turn, carry):
        j = lax.rem(turn + lax.rem(right // 2, chips), half)
        ring_two(half * core + j).start()
        ring_two(half * (1 - core) + j).start()
        return carry

    for s in reversed(range(slots)):
        if s == 0:
            ring_one.wait_recv()
        if s == last:
            advance(relaxed.at[s], sent.at[1], first_slice + s)
            lax.fori_loop(0, half, send_two, 0)
        else:
            advance(relaxed.at[s], previous.at[s + 1], first_slice + s)

    def make_maps(t):
        here = pl.ds(pl.multiple_of(ROWS * t, ROWS), ROWS)
        for k in range(3):
            whole = None
            for s in range(slots):
                mapping = slot_map(
                    previous[s, 0, k, here], previous[s, 1, k, here],
                    relaxed[s, 0, k, here], relaxed[s, 1, k, here],
                )
                for n in range(5):
                    maps[s, t, n, k] = mapping[n]
                whole = mapping if whole is None else compose(whole, mapping)
            for n in range(5):
                own[t, n, k] = whole[n]

    def fields(ref, *place):
        return tuple(ref[(*place, n)] for n in range(5))

    def a_copy(j):
        return remote(
            own.at[half * (1 - core) + j], got.at[j], a_s.at[j], a_r.at[j], partner
        )

    def owner_of(j):
        return j + (j + half - 1) // half + (j + 1) // half

    def b_copy(j):
        return remote(
            pair.at[j], parts.at[chip], b_s.at[j], b_r.at[chip],
            base + 2 * owner_of(j) + core,
        )

    def pair_step(turn):
        j = lax.rem(turn + chip, half)
        a_copy(j).wait_recv()
        for k in range(3):
            mine = tuple(own[half * core + j, n, k] for n in range(5))
            theirs = tuple(got[j, n, k] for n in range(5))
            is_first = core == 0
            earlier = tuple(jnp.where(is_first, m, h) for m, h in zip(mine, theirs))
            later = tuple(jnp.where(is_first, h, m) for m, h in zip(mine, theirs))
            both = compose(earlier, later)
            for n in range(5):
                early[j, n, k] = earlier[n]
                pair[j, n, k] = both[n]

        @pl.when(owner_of(j) != chip)
        def _():
            b_copy(j).start()

        @pl.when(owner_of(j) == chip)
        def _():
            parts[chip] = pair[j]

    def phase_maps(turn, carry):
        j = lax.rem(turn + chip, half)
        away, mine = half * (1 - core) + j, half * core + j
        ring_two(away).wait_recv()
        make_maps(away)
        a_copy(j).start()
        ring_two(mine).wait_recv()
        make_maps(mine)

        @pl.when(turn > 0)
        def _():
            pair_step(turn - 1)

        return carry

    lax.fori_loop(0, half, phase_maps, 0)
    pair_step(half - 1)

    def c_copy(k):
        return remote(
            leave.at[k], enter.at[my_tile], c_s.at[k], c_r.at[my_tile], base + 2 * k + core
        )

    @pl.when(owner)
    def _():
        for k in range(chips):
            @pl.when(chip != k)
            def _():
                remote(
                    pair.at[0], parts.at[k], b_s.at[0], b_r.at[k], base + 2 * k + core
                ).wait_recv()

        whole = fields(parts, 0)
        for k in range(1, chips):
            whole = compose(whole, fields(parts, k))
        if groups == 1:
            state = loop_point(whole)
        else:
            total[...] = jnp.stack(whole)
            totals[group] = total[...]

            def g_copy(hop):
                to = lax.rem(me + hop * 2 * chips, loop_size)
                return remote(total, totals.at[group], g_s.at[hop], g_r.at[hop], to)

            for hop in range(1, groups):
                g_copy(hop).start()
            for hop in range(1, groups):
                g_copy(hop).wait()
            whole = fields(totals, 0)
            for g in range(1, groups):
                whole = compose(whole, fields(totals, g))
            state = loop_point(whole)
            for g in range(groups - 1):
                after = apply_map(fields(totals, g), state[0], state[1])
                state = tuple(jnp.where(g < group, n, o) for n, o in zip(after, state))
        for k in range(chips):
            leave[k, 0] = state[0]
            leave[k, 1] = state[1]

            @pl.when(chip != k)
            def _():
                c_copy(k).start()

            @pl.when(chip == k)
            def _():
                enter[my_tile] = leave[k]

            if k < chips - 1:
                state = apply_map(fields(parts, k), state[0], state[1])

    def finish(t):
        here = pl.ds(pl.multiple_of(ROWS * t, ROWS), ROWS)
        for k in range(3):
            value = (entry[t, 0, k], entry[t, 1, k])
            for s in range(slots):
                mapping = tuple(maps[s, t, n, k] for n in range(5))
                value = apply_map(mapping, value[0], value[1])
                out_ref[s, 0, k, here] = relaxed[s, 0, k, here] + value[0]
                out_ref[s, 1, k, here] = relaxed[s, 1, k, here] + value[1]

    def d_copy(j):
        return remote(pass_on.at[j], entry.at[half * core + j], d_s.at[j], d_r.at[j], partner)

    def phase_back(j, carry):
        @pl.when(owner_of(j) != chip)
        def _():
            remote(
                leave.at[0], enter.at[j], c_s.at[0], c_r.at[j], base + 2 * owner_of(j) + core
            ).wait_recv()

        for k in range(3):
            zero = (enter[j, 0, k], enter[j, 1, k])
            one = apply_map(tuple(early[j, n, k] for n in range(5)), zero[0], zero[1])
            for n in range(2):
                entry[half * core + j, n, k] = jnp.where(core == 0, zero[n], one[n])
                pass_on[j, n, k] = jnp.where(core == 0, one[n], zero[n])
        d_copy(j).start()
        finish(half * core + j)
        return carry

    lax.fori_loop(0, half, phase_back, 0)

    def phase_theirs(j, carry):
        remote(
            pass_on.at[j], entry.at[half * (1 - core) + j], d_s.at[j], d_r.at[j], partner
        ).wait_recv()
        finish(half * (1 - core) + j)
        return carry

    lax.fori_loop(0, half, phase_theirs, 0)

    ring_one.wait_send()
    for t in range(tiles):
        ring_two(t).wait_send()
    for j in range(half):
        a_copy(j).wait_send()
        d_copy(j).wait_send()

        @pl.when(owner_of(j) != chip)
        def _():
            b_copy(j).wait_send()

    @pl.when(owner)
    def _():
        for k in range(chips):
            @pl.when(chip != k)
            def _():
                c_copy(k).wait_send()


def unpack(packed):
    rest = packed[..., 2, :, :]
    rest = jnp.stack([rest[..., : LANES // 2], rest[..., LANES // 2 :]], axis=-3)
    return jnp.concatenate([packed[..., :2, :, :], rest], axis=-1)


def on_device(iterate, labels, stim_mask):
    loop_size = lax.axis_size("tm")
    chips = 8
    groups = loop_size // (2 * chips)
    slots = iterate.shape[0]
    rows = labels.shape[1]
    tiles = rows // ROWS
    half = tiles // 2
    f32 = jnp.float32
    state = (slots, 2, 3, rows, LANES)
    block = (3, ROWS, LANES)
    dma = pltpu.SemaphoreType.DMA
    out = pl.pallas_call(
        functools.partial(kernel, loop_size, chips, groups),
        out_shape=jax.ShapeDtypeStruct(state, f32),
        in_specs=[pl.BlockSpec(memory_space=pl.ANY)] * 3,
        out_specs=pl.BlockSpec(memory_space=pltpu.VMEM),
        scratch_shapes=[
            pltpu.VMEM(iterate.shape, f32),
            pltpu.VMEM(labels.shape, labels.dtype),
            pltpu.VMEM(stim_mask.shape, stim_mask.dtype),
            pltpu.VMEM(state, f32),
            pltpu.VMEM((3, rows, LANES), f32),
            pltpu.SemaphoreType.DMA((slots + 2,)),
            pltpu.VMEM((2, 3, rows + 2 * ROWS, LANES), f32),
            pltpu.VMEM((3, rows, LANES), f32),
            pltpu.VMEM((3, rows, LANES), f32),
            pltpu.VMEM((1, 3, rows + 2 * ROWS, LANES), f32),
            pltpu.VMEM((6, 3, rows, LANES), f32),
            pltpu.VMEM(state, f32),
            pltpu.VMEM(state, f32),
            pltpu.VMEM((2, 2, 3, rows, LANES), f32),
            pltpu.VMEM((slots, tiles, 5) + block, f32),
            pltpu.VMEM((tiles, 5) + block, f32),
            pltpu.VMEM((half, 5) + block, f32),
            pltpu.VMEM((half, 5) + block, f32),
            pltpu.VMEM((half, 5) + block, f32),
            pltpu.VMEM((chips, 5) + block, f32),
            pltpu.VMEM((5,) + block, f32),
            pltpu.VMEM((groups, 5) + block, f32),
            pltpu.VMEM((chips, 2) + block, f32),
            pltpu.VMEM((half, 2) + block, f32),
            pltpu.VMEM((half, 2) + block, f32),
            pltpu.VMEM((tiles, 2) + block, f32),
            dma((1 + tiles,)), dma((1 + tiles,)),
            dma((half,)), dma((half,)),
            dma((half,)), dma((chips,)),
            dma((groups,)), dma((groups,)),
            dma((chips,)), dma((half,)),
            dma((half,)), dma((half,)),
        ],
        compiler_params=pltpu.CompilerParams(
            collective_id=0, has_side_effects=True, vmem_limit_bytes=32 * 1024 * 1024
        ),
    )(iterate, labels, stim_mask)
    return unpack(out)


def solution(mesh):
    in_specs = (
        P(("group", "tm"), None, None, None, None),
        P("group", None, None),
        P("group", None, None),
    )
    out_specs = P(("group", "tm"), None, None, None, None)
    return jax.shard_map(
        on_device, mesh=mesh, in_specs=in_specs, out_specs=out_specs, check_vma=False
    )
```

```python
import functools

import jax
import jax.numpy as jnp
from jax import lax
from jax.experimental import pallas as pl
from jax.experimental.pallas import tpu as pltpu
from jax.sharding import PartitionSpec as P

MSTEPS = 8
PULSE = 16
LANES = 128
ROWS = 8

time_step = 0.05
excite_gain = 8.0
threshold = 0.15
recovery_base = 0.005
recovery_gain = 0.2
recovery_shift = 0.3
pulse_height = 1.0
coarse_floor = -0.5
conduct_table = (0.1, 0.35, 0.7, 1.0)


def inverse(value):
    guess = pl.reciprocal(value, approx=True)
    return guess * (2.0 - value * guess)


def scaled_rate(potential, recovery, scale):
    above = (scale * recovery_gain) * jnp.maximum(recovery, 0.0)
    return scale * recovery_base + above * inverse(jnp.maximum(potential, 0.0) + recovery_shift)


def compose(earlier, latter):
    return (
        latter[0] * earlier[0],
        latter[1] * earlier[0] + latter[2] * earlier[1],
        latter[2] * earlier[2],
        latter[0] * earlier[3] + latter[3],
        latter[1] * earlier[3] + latter[2] * earlier[4] + latter[4],
    )


def apply_map(mapping, first_in, second_in):
    return (
        mapping[0] * first_in + mapping[3],
        mapping[1] * first_in + mapping[2] * second_in + mapping[4],
    )


def loop_point(loop_map):
    first_part = loop_map[3] / (1.0 - loop_map[0])
    second = (loop_map[4] + loop_map[1] * first_part) / (1.0 - loop_map[2])
    return (first_part, second)


def neighbours(ref, slot, tile, lane):
    here = pl.ds(ROWS + ROWS * tile, ROWS)
    above = pl.ds(ROWS - 1 + ROWS * tile, ROWS)
    below = pl.ds(ROWS + 1 + ROWS * tile, ROWS)
    mid = [ref[slot, k, here] for k in range(3)]
    up = [ref[slot, k, above] for k in range(3)]
    down = [ref[slot, k, below] for k in range(3)]
    first, second, rest = mid
    swapped = pltpu.roll(rest, 64, 1)
    first_left = pltpu.roll(first, 1, 1)
    rest_right = pltpu.roll(rest, LANES - 1, 1)
    left = [
        first_left,
        pltpu.roll(second, 1, 1),
        jnp.where(
            lane == 0,
            first_left,
            jnp.where(lane == 64, pltpu.roll(second, 65, 1), pltpu.roll(rest, 1, 1)),
        ),
    ]
    right = [
        jnp.where(lane == LANES - 1, rest_right, pltpu.roll(first, LANES - 1, 1)),
        jnp.where(
            lane == LANES - 1,
            pltpu.roll(swapped, LANES - 1, 1),
            pltpu.roll(second, LANES - 1, 1),
        ),
        rest_right,
    ]
    return mid, up, down, left, right, [second, first, swapped]


def packed(ref, place, here):
    first, second = ref[(*place, 0, here)], ref[(*place, 1, here)]
    rest = jnp.concatenate([first[:, LANES:], second[:, LANES:]], axis=1)
    return [first[:, :LANES], second[:, :LANES], rest]


def slot_map(prev_p, prev_q, relax_p, relax_q):
    potential = jnp.clip(prev_p, 0.0, 1.0)
    recovery = jnp.maximum(prev_q, 0.0)
    recover_rate = scaled_rate(potential, recovery, 1.0)
    horizon = MSTEPS * time_step
    fast_slope = jnp.minimum(
        -excite_gain
        * (3.0 * potential * potential - 2.0 * (1.0 + threshold) * potential + threshold)
        - recovery,
        coarse_floor,
    )
    cross_term = -recover_rate * excite_gain * (2.0 * potential - threshold - 1.0)
    first_diag = inverse(1.0 - horizon * fast_slope)
    second_diag = inverse(1.0 + horizon * recover_rate)
    lower_term = horizon * cross_term * first_diag * second_diag
    return (first_diag, lower_term, second_diag, prev_p - relax_p, prev_q - relax_q)


def kernel(
    loop_size, chips, groups,
    iterate_hbm, labels_hbm, stim_hbm, out_ref,
    raw, raw_labels, raw_stim, it_ref, stim_ref, load_sem,
    pot, rec, drive, cond, coef, relaxed, previous, sent, maps, own, got, early, pair,
    parts, total, totals, leave, enter, pass_on, entry,
    ring_s, ring_r, a_s, a_r, b_s, b_r, g_s, g_r, c_s, c_r, d_s, d_r,
):
    slots = it_ref.shape[0]
    tiles = stim_ref.shape[1] // ROWS
    last = slots - 1
    loads = [
        pltpu.make_async_copy(labels_hbm, raw_labels, load_sem.at[slots]),
        pltpu.make_async_copy(stim_hbm, raw_stim, load_sem.at[slots + 1]),
    ]
    for s in reversed(range(slots)):
        loads.append(pltpu.make_async_copy(iterate_hbm.at[s], raw.at[s], load_sem.at[s]))
    half = tiles // 2
    me = lax.axis_index("tm")
    core = lax.rem(me, 2)
    chip = lax.rem(me // 2, chips)
    group = me // (2 * chips)
    base = group * 2 * chips
    partner = me + 1 - 2 * core
    right = lax.rem(me + 1, loop_size)
    across = lax.rem(me + 2 * core - 1 + loop_size, loop_size)
    owner = jnp.logical_and(chip != 1, chip != chips - 2)
    my_tile = chip - (chip + chips - 1) // chips - (chip + 2) // chips

    barrier = pltpu.get_barrier_semaphore()

    def greet(device):
        pl.semaphore_signal(
            barrier, inc=1, device_id={"tm": device}, device_id_type=pl.DeviceIdType.MESH
        )

    greet(partner)
    greet(across)
    for hop in range(1, chips):
        greet(base + 2 * lax.rem(chip + hop, chips) + core)
    for hop in range(1, groups):
        greet(lax.rem(me + hop * 2 * chips, loop_size))

    def remote(source, target, send_sem, recv_sem, device):
        return pltpu.make_async_remote_copy(
            src_ref=source, dst_ref=target, send_sem=send_sem, recv_sem=recv_sem,
            device_id={"tm": device}, device_id_type=pl.DeviceIdType.MESH,
        )

    for load in loads:
        load.start()

    lane = lax.broadcasted_iota(jnp.int32, (ROWS, LANES), 1)
    row = lax.broadcasted_iota(jnp.int32, (ROWS, LANES), 0)
    edge = jnp.zeros((ROWS, LANES), jnp.float32)
    for k in range(3):
        for end in (0, ROWS + ROWS * tiles):
            cond[0, k, pl.ds(end, ROWS)] = edge
            pot[0, k, pl.ds(end, ROWS)] = edge
            pot[1, k, pl.ds(end, ROWS)] = edge
    loads[0].wait()
    for t in range(tiles):
        here = pl.ds(ROWS * t, ROWS)
        for k, label in enumerate(packed(raw_labels, (), here)):
            conduct = jnp.full((ROWS, LANES), conduct_table[0], jnp.float32)
            for label_id in range(1, len(conduct_table)):
                conduct = jnp.where(label == label_id, conduct_table[label_id], conduct)
            cond[0, k, pl.ds(ROWS + ROWS * t, ROWS)] = conduct
    loads[1].wait()
    for t in range(tiles):
        here = pl.ds(ROWS * t, ROWS)
        for k, mask in enumerate(packed(raw_stim, (), here)):
            stim_ref[k, here] = mask.astype(jnp.float32)
    for t in range(tiles):
        mid, up, down, left, right_, over = neighbours(cond, 0, t, lane)
        here = pl.ds(ROWS * t, ROWS)
        for k in range(3):
            def face(value, open_face=None):
                mean = time_step * 0.5 * (mid[k] + value)
                return mean if open_face is None else jnp.where(open_face, mean, 0.0)

            faces = (
                face(up[k], row > 0 if t == 0 else None),
                face(down[k], row < ROWS - 1 if t == tiles - 1 else None),
                face(left[k], lane > 0 if k < 2 else None),
                face(
                    right_[k],
                    None if k < 2 else jnp.logical_and(lane != 63, lane != LANES - 1),
                ),
                face(over[k]),
            )
            for n, value in enumerate(faces):
                coef[n, k, here] = value
            stay = 1.0 - time_step * excite_gain * threshold
            coef[5, k, here] = stay - (((faces[0] + faces[1]) + (faces[2] + faces[3])) + faces[4])

    def unload(s):
        loads[2 + last - s].wait()
        for n in range(2):
            for t in range(tiles):
                here = pl.ds(ROWS * t, ROWS)
                for k, value in enumerate(packed(raw, (s, n), here)):
                    it_ref[s, n, k, here] = value

    def advance(source, target, slice_index):
        switch = jnp.where(slice_index * MSTEPS < PULSE, time_step * pulse_height, 0.0)
        for k in range(3):
            pot[0, k, pl.ds(ROWS, ROWS * tiles)] = source[0, k]
            rec[k] = source[1, k]
            drive[k] = switch * stim_ref[k]

        def two_steps(turn, carry):
            for now in (0, 1):
                for t in range(tiles):
                    mid, up, down, left, right_, over = neighbours(pot, now, t, lane)
                    here = pl.ds(ROWS * t, ROWS)
                    for k in range(3):
                        p, q = mid[k], rec[k, here]
                        flow = coef[0, k, here] * up[k] + coef[1, k, here] * down[k]
                        flow = flow + (coef[2, k, here] * left[k] + coef[3, k, here] * right_[k])
                        flow = flow + (coef[4, k, here] * over[k] + drive[k, here])
                        pull = q + excite_gain * (p * (p - (threshold + 1.0)))
                        keep = coef[5, k, here] - time_step * pull
                        pot[1 - now, k, pl.ds(ROWS + ROWS * t, ROWS)] = p * keep + flow
                        rec[k, here] = q - scaled_rate(p, q, time_step) * pull
            return carry

        lax.fori_loop(0, MSTEPS // 2, two_steps, 0)
        for k in range(3):
            target[0, k] = pot[0, k, pl.ds(ROWS, ROWS * tiles)]
            target[1, k] = rec[k]

    first_slice = me * slots
    unload(last)
    advance(it_ref.at[last], sent.at[0], first_slice + last)
    pl.semaphore_wait(barrier, chips + 1 + groups - 1)
    ring_one = [
        remote(
            sent.at[0, n], relaxed.at[0, n], ring_s.at[n * (1 + tiles)],
            ring_r.at[n * (1 + tiles)], right,
        )
        for n in range(2)
    ]
    for copy in ring_one:
        copy.start()
    for s in reversed(range(last)):
        unload(s)
        advance(it_ref.at[s], relaxed.at[s + 1], first_slice + s)

    def ring_two(t):
        here = pl.ds(pl.multiple_of(ROWS * t, ROWS), ROWS)
        return remote(
            sent.at[1, :, :, here], previous.at[0, :, :, here],
            ring_s.at[1 + t], ring_r.at[1 + t], right,
        )

    def send_two(turn, carry):
        j = lax.rem(turn + lax.rem(right // 2, chips), half)
        ring_two(half * core + j).start()
        ring_two(half * (1 - core) + j).start()
        return carry

    for s in reversed(range(slots)):
        if s == 0:
            for copy in ring_one:
                copy.wait_recv()
        if s == last:
            advance(relaxed.at[s], sent.at[1], first_slice + s)
            lax.fori_loop(0, half, send_two, 0)
        else:
            advance(relaxed.at[s], previous.at[s + 1], first_slice + s)

    def make_maps(t):
        here = pl.ds(pl.multiple_of(ROWS * t, ROWS), ROWS)
        for k in range(3):
            whole = None
            for s in range(slots):
                mapping = slot_map(
                    previous[s, 0, k, here], previous[s, 1, k, here],
                    relaxed[s, 0, k, here], relaxed[s, 1, k, here],
                )
                for n in range(5):
                    maps[s, t, n, k] = mapping[n]
                whole = mapping if whole is None else compose(whole, mapping)
            for n in range(5):
                own[t, n, k] = whole[n]

    def fields(ref, *place):
        return tuple(ref[(*place, n)] for n in range(5))

    def a_copy(j):
        return remote(
            own.at[half * (1 - core) + j], got.at[j], a_s.at[j], a_r.at[j], partner
        )

    def owner_of(j):
        return j + (j + half - 1) // half + (j + 1) // half

    def b_copy(j):
        return remote(
            pair.at[j], parts.at[chip], b_s.at[j], b_r.at[chip],
            base + 2 * owner_of(j) + core,
        )

    def pair_step(turn):
        j = lax.rem(turn + chip, half)
        a_copy(j).wait_recv()
        for k in range(3):
            mine = tuple(own[half * core + j, n, k] for n in range(5))
            theirs = tuple(got[j, n, k] for n in range(5))
            is_first = core == 0
            earlier = tuple(jnp.where(is_first, m, h) for m, h in zip(mine, theirs))
            later = tuple(jnp.where(is_first, h, m) for m, h in zip(mine, theirs))
            both = compose(earlier, later)
            for n in range(5):
                early[j, n, k] = earlier[n]
                pair[j, n, k] = both[n]

        @pl.when(owner_of(j) != chip)
        def _():
            b_copy(j).start()

        @pl.when(owner_of(j) == chip)
        def _():
            parts[chip] = pair[j]

    def phase_maps(turn, carry):
        j = lax.rem(turn + chip, half)
        away, mine = half * (1 - core) + j, half * core + j
        ring_two(away).wait_recv()
        make_maps(away)
        a_copy(j).start()
        ring_two(mine).wait_recv()
        make_maps(mine)

        @pl.when(turn > 0)
        def _():
            pair_step(turn - 1)

        return carry

    lax.fori_loop(0, half, phase_maps, 0)
    pair_step(half - 1)

    def c_copy(k):
        return remote(
            leave.at[k], enter.at[my_tile], c_s.at[k], c_r.at[my_tile], base + 2 * k + core
        )

    @pl.when(owner)
    def _():
        for k in range(chips):
            @pl.when(chip != k)
            def _():
                remote(
                    pair.at[0], parts.at[k], b_s.at[0], b_r.at[k], base + 2 * k + core
                ).wait_recv()

        whole = fields(parts, 0)
        for k in range(1, chips):
            whole = compose(whole, fields(parts, k))
        if groups == 1:
            state = loop_point(whole)
        else:
            total[...] = jnp.stack(whole)
            totals[group] = total[...]

            def g_copy(hop):
                to = lax.rem(me + hop * 2 * chips, loop_size)
                return remote(total, totals.at[group], g_s.at[hop], g_r.at[hop], to)

            for hop in range(1, groups):
                g_copy(hop).start()
            for hop in range(1, groups):
                g_copy(hop).wait()
            whole = fields(totals, 0)
            for g in range(1, groups):
                whole = compose(whole, fields(totals, g))
            state = loop_point(whole)
            for g in range(groups - 1):
                after = apply_map(fields(totals, g), state[0], state[1])
                state = tuple(jnp.where(g < group, n, o) for n, o in zip(after, state))
        for k in range(chips):
            leave[k, 0] = state[0]
            leave[k, 1] = state[1]

            @pl.when(chip != k)
            def _():
                c_copy(k).start()

            @pl.when(chip == k)
            def _():
                enter[my_tile] = leave[k]

            if k < chips - 1:
                state = apply_map(fields(parts, k), state[0], state[1])

    def finish(t):
        here = pl.ds(pl.multiple_of(ROWS * t, ROWS), ROWS)
        for k in range(3):
            value = (entry[t, 0, k], entry[t, 1, k])
            for s in range(slots):
                mapping = tuple(maps[s, t, n, k] for n in range(5))
                value = apply_map(mapping, value[0], value[1])
                out_ref[s, 0, k, here] = relaxed[s, 0, k, here] + value[0]
                out_ref[s, 1, k, here] = relaxed[s, 1, k, here] + value[1]

    def d_copy(j):
        return remote(pass_on.at[j], entry.at[half * core + j], d_s.at[j], d_r.at[j], partner)

    def phase_back(j, carry):
        @pl.when(owner_of(j) != chip)
        def _():
            remote(
                leave.at[0], enter.at[j], c_s.at[0], c_r.at[j], base + 2 * owner_of(j) + core
            ).wait_recv()

        for k in range(3):
            zero = (enter[j, 0, k], enter[j, 1, k])
            one = apply_map(tuple(early[j, n, k] for n in range(5)), zero[0], zero[1])
            for n in range(2):
                entry[half * core + j, n, k] = jnp.where(core == 0, zero[n], one[n])
                pass_on[j, n, k] = jnp.where(core == 0, one[n], zero[n])
        d_copy(j).start()
        finish(half * core + j)
        return carry

    lax.fori_loop(0, half, phase_back, 0)

    def phase_theirs(j, carry):
        remote(
            pass_on.at[j], entry.at[half * (1 - core) + j], d_s.at[j], d_r.at[j], partner
        ).wait_recv()
        finish(half * (1 - core) + j)
        return carry

    lax.fori_loop(0, half, phase_theirs, 0)

    for copy in ring_one:
        copy.wait_send()
    for t in range(tiles):
        ring_two(t).wait_send()
    for j in range(half):
        a_copy(j).wait_send()
        d_copy(j).wait_send()

        @pl.when(owner_of(j) != chip)
        def _():
            b_copy(j).wait_send()

    @pl.when(owner)
    def _():
        for k in range(chips):
            @pl.when(chip != k)
            def _():
                c_copy(k).wait_send()


def unpack(packed):
    rest = packed[..., 2, :, :]
    rest = jnp.stack([rest[..., : LANES // 2], rest[..., LANES // 2 :]], axis=-3)
    return jnp.concatenate([packed[..., :2, :, :], rest], axis=-1)


def on_device(iterate, labels, stim_mask):
    loop_size = lax.axis_size("tm")
    chips = 8
    groups = loop_size // (2 * chips)
    slots = iterate.shape[0]
    rows = labels.shape[1]
    tiles = rows // ROWS
    half = tiles // 2
    f32 = jnp.float32
    state = (slots, 2, 3, rows, LANES)
    block = (3, ROWS, LANES)
    dma = pltpu.SemaphoreType.DMA
    out = pl.pallas_call(
        functools.partial(kernel, loop_size, chips, groups),
        out_shape=jax.ShapeDtypeStruct(state, f32),
        in_specs=[pl.BlockSpec(memory_space=pl.ANY)] * 3,
        out_specs=pl.BlockSpec(memory_space=pltpu.VMEM),
        scratch_shapes=[
            pltpu.VMEM(iterate.shape, f32),
            pltpu.VMEM(labels.shape, labels.dtype),
            pltpu.VMEM(stim_mask.shape, stim_mask.dtype),
            pltpu.VMEM(state, f32),
            pltpu.VMEM((3, rows, LANES), f32),
            pltpu.SemaphoreType.DMA((slots + 2,)),
            pltpu.VMEM((2, 3, rows + 2 * ROWS, LANES), f32),
            pltpu.VMEM((3, rows, LANES), f32),
            pltpu.VMEM((3, rows, LANES), f32),
            pltpu.VMEM((1, 3, rows + 2 * ROWS, LANES), f32),
            pltpu.VMEM((6, 3, rows, LANES), f32),
            pltpu.VMEM(state, f32),
            pltpu.VMEM(state, f32),
            pltpu.VMEM((2, 2, 3, rows, LANES), f32),
            pltpu.VMEM((slots, tiles, 5) + block, f32),
            pltpu.VMEM((tiles, 5) + block, f32),
            pltpu.VMEM((half, 5) + block, f32),
            pltpu.VMEM((half, 5) + block, f32),
            pltpu.VMEM((half, 5) + block, f32),
            pltpu.VMEM((chips, 5) + block, f32),
            pltpu.VMEM((5,) + block, f32),
            pltpu.VMEM((groups, 5) + block, f32),
            pltpu.VMEM((chips, 2) + block, f32),
            pltpu.VMEM((half, 2) + block, f32),
            pltpu.VMEM((half, 2) + block, f32),
            pltpu.VMEM((tiles, 2) + block, f32),
            dma((2 + tiles,)), dma((2 + tiles,)),
            dma((half,)), dma((half,)),
            dma((half,)), dma((chips,)),
            dma((groups,)), dma((groups,)),
            dma((chips,)), dma((half,)),
            dma((half,)), dma((half,)),
        ],
        compiler_params=pltpu.CompilerParams(
            collective_id=0, has_side_effects=True, vmem_limit_bytes=32 * 1024 * 1024
        ),
    )(iterate, labels, stim_mask)
    return unpack(out)


def solution(mesh):
    in_specs = (
        P(("group", "tm"), None, None, None, None),
        P("group", None, None),
        P("group", None, None),
    )
    out_specs = P(("group", "tm"), None, None, None, None)
    return jax.shard_map(
        on_device, mesh=mesh, in_specs=in_specs, out_specs=out_specs, check_vma=False
    )
```
